512 devices in a mesh: tile: 64 (over x, z), head: 8 (over y, core).
Axes of the slice: x: 4, y: 4, z: 16, core: 2. Of those that a mesh axis runs over, the one named last changes fastest.
Arguments:
- queries: bfloat16 [16384, 2048], P('tile', 'head'), may hold values from -26.5 to 26.5
- keys: bfloat16 [16384, 2048], P('tile', 'head'), may hold values from -26.5 to 26.5
- values: bfloat16 [16384, 2048], P('tile', 'head'), may hold values from -36 to 36
- out_weight: bfloat16 [2048, 2048], P('head'), may hold values from -0.1875 to 0.1875
- teacher: bfloat16 [16384, 2048], P('tile', 'head'), may hold values from -3 to 3
- block_lists: int32 [16, 64, 27], P('head', 'tile'), may hold values from -1 to 63, as said below
Outputs:
- student: bfloat16 [16384, 2048], P('tile', 'head')
- grad_queries: bfloat16 [16384, 2048], P('tile', 'head')
- grad_keys: bfloat16 [16384, 2048], P('tile', 'head')
- grad_values: bfloat16 [16384, 2048], P('tile', 'head')
The draws below stay inside these ranges and needn't reach their ends.
Inputs may be any that keep to these rules, and one draw needn't show every extreme that they name: `block_lists`: tile c has grid coordinates (c // 32, (c // 8) % 4, c % 8) in a 2 x 4 x 8 grid. Row (h, c) lists, each at most once, tiles within one step of tile c along each of the three grid dimensions; tile c itself is always listed; the other slots hold -1.
All inputs are finite; a program needn't handle non-finite values.
Results may differ from the reference program's by a relative error of at most 0.035.
Values may be sent and summed in bfloat16 or wider, within the bound.
No kernel may reach another device: no remote copies, remote signals or barrier semaphores. Data moves between devices by JAX's collectives and lax.ppermute only.
A program may use at most 64 MiB of HBM per device.

```python
import jax
import jax.numpy as jnp
from jax import lax

HEADS = 16
HD = 128
D = 2048
TW = 8
WINDOW = 27
TILE = 256
TILES = 64
TOKENS = 16384
N_HEAD = 8


def draw_queries(key, part):
    key = jax.random.fold_in(key, 11)
    noise = 1.3 * jnp.clip(jax.random.normal(key, (TOKENS, D), jnp.float32), -6.0, 6.0)
    return noise.astype(jnp.bfloat16)


def draw_keys(key, part):
    key = jax.random.fold_in(key, 13)
    noise = 1.3 * jnp.clip(jax.random.normal(key, (TOKENS, D), jnp.float32), -6.0, 6.0)
    return noise.astype(jnp.bfloat16)


def draw_block_lists(key, part):
    key = jax.random.fold_in(key, 7)
    level_key, roll_key = jax.random.split(key)
    half = TILES // 2
    rows_total = half // TW
    tile_ids = jnp.arange(TILES, dtype=jnp.int32)
    frame = tile_ids // half
    grid_row = tile_ids % half // TW
    grid_col = tile_ids % TW
    step_frame = jnp.array([a for a in (-1, 0, 1) for b in (-1, 0, 1) for c in (-1, 0, 1)], jnp.int32)
    step_row = jnp.array([b for a in (-1, 0, 1) for b in (-1, 0, 1) for c in (-1, 0, 1)], jnp.int32)
    step_col = jnp.array([c for a in (-1, 0, 1) for b in (-1, 0, 1) for c in (-1, 0, 1)], jnp.int32)
    new_frame = frame[:, None] + step_frame[None, :]
    new_row = grid_row[:, None] + step_row[None, :]
    new_col = grid_col[:, None] + step_col[None, :]
    inside = (new_frame >= 0) & (new_frame < 2) & (new_row >= 0) & (new_row < rows_total) & (new_col >= 0) & (new_col < TW)
    neighbour = new_frame * half + new_row * TW + new_col
    levels = jax.random.randint(level_key, (HEADS, 1, 1), 1, 5)
    rolled = jax.random.randint(roll_key, (HEADS, TILES, WINDOW), 0, 4)
    centre = (jnp.arange(WINDOW) == 13)[None, None, :]
    keep = (rolled < levels) | centre
    return jnp.where(inside[None] & keep, neighbour[None], -1).astype(jnp.int32)


def strengthened(values, stream_key, source, target, parts, factor):
    owner, partner = [(jnp.arange(values.shape[dim]) // (values.shape[dim] // parts)).reshape([-1 if axis == dim else 1 for axis in range(values.ndim)]) for dim in (source, target)]
    chosen = jax.random.permutation(stream_key, parts)[partner]
    strong = (owner == chosen) | (owner == (partner + parts // 2) % parts)
    return jnp.where(strong, factor * values, values)


def steps_of(key, shape, pieces, low, top_value):
    level = 1.0
    for dim, shards_of in pieces:
        heights = jax.random.uniform(jax.random.fold_in(jax.random.fold_in(key, 6), dim), (shards_of,), jnp.float32, low / len(pieces), top_value / len(pieces))
        level = level * jnp.repeat(jnp.exp(heights), shape[dim] // shards_of).reshape((-1,) + (1,) * (len(shape) - 1 - dim))
    return level


def scatter_about(stream_key, extent, spread, most, cuts=(), kind=jnp.bfloat16):
    gain = steps_of(stream_key, extent, cuts, -0.22, 0.18) if cuts else 1.0
    entries = jax.random.normal(stream_key, extent, jnp.float32) * spread * gain
    return jnp.minimum(jnp.maximum(entries, -most), most).astype(kind)


def noise_with(key, dims, width, most, pieces, heavy, kind=jnp.bfloat16):
    drawn = width * jax.random.normal(key, dims, jnp.float32)
    if pieces:
        drawn = drawn * steps_of(key, dims, pieces, -0.22, 0.18)
    return jnp.clip(strengthened(drawn, jax.random.fold_in(key, 3), *heavy), -most, most).astype(kind)


def setup_inputs(seed: int = 0) -> dict:
    key_list = jax.random.split(jax.random.key(seed), 7)
    return {
        "queries": draw_queries(jax.random.fold_in(key_list[6], 71), 0),
        "keys": draw_keys(jax.random.fold_in(key_list[6], 71), 0),
        "values": scatter_about(key_list[2], (TOKENS, D), 6.0, 36.0, ((0, 64), (1, 8))),
        "out_weight": noise_with(key_list[3], (D, D), D ** -0.5, 0.1875, ((0, 8),), (0, 1, 8, 2.0)),
        "teacher": scatter_about(key_list[4], (TOKENS, D), 0.5, 3.0, ((0, 64), (1, 8))),
        "block_lists": draw_block_lists(jax.random.fold_in(key_list[6], 71), 0),
    }


def heads_first(matrix):
    return matrix.reshape(TILES, TILE, HEADS, HD).transpose(2, 0, 1, 3)


def carry_to_tokens(blocks):
    return blocks.transpose(1, 2, 0, 3).reshape(TOKENS, HEADS * HD)


def mapped_to_tokens(blocks):
    return blocks.transpose(0, 2, 1, 3).reshape(TOKENS, HEADS * HD)


def settle(matrix):
    return lax.optimization_barrier(matrix.astype(jnp.bfloat16)).astype(jnp.float32)


def reference(queries, keys, values, out_weight, teacher, block_lists):
    score_scale = HD ** -0.5
    query_blocks = heads_first(queries)
    key_blocks = heads_first(keys)
    value_blocks = heads_first(values)
    tile_order = jnp.arange(TILES, dtype=jnp.int32)

    def gather_tiles(blocks, safe_ids):
        return jax.vmap(lambda per_head, head_ids: per_head[head_ids])(blocks, safe_ids)

    def forward_tile(tile_index):
        listed_ids = block_lists[:, tile_index, :]
        live_slots = listed_ids >= 0
        safe_ids = jnp.where(live_slots, listed_ids, 0).astype(jnp.int32)
        key_tiles = gather_tiles(key_blocks, safe_ids).astype(jnp.float32)
        value_tiles = gather_tiles(value_blocks, safe_ids).astype(jnp.float32)
        query_tile = query_blocks[:, tile_index].astype(jnp.float32)
        scores = jnp.einsum("hqd,hnkd->hqnk", query_tile, key_tiles) * score_scale
        scores = jnp.where(live_slots[:, None, :, None], scores, -jnp.inf)
        highest = jnp.max(scores, axis=(2, 3), keepdims=True)
        weights = jnp.exp(scores - highest)
        probs_low = settle(weights / jnp.sum(weights, axis=(2, 3), keepdims=True))
        attended_tile = jnp.einsum("hqnk,hnkd->hqd", probs_low, value_tiles).astype(jnp.bfloat16)
        return query_tile, key_tiles, value_tiles, listed_ids, live_slots, probs_low, attended_tile

    attended = mapped_to_tokens(lax.map(lambda tile_index: forward_tile(tile_index)[6], tile_order))

    group_width = D // N_HEAD
    total = jnp.zeros((TOKENS, D), jnp.float32)
    for group in range(N_HEAD):
        product = jnp.dot(attended[:, group * group_width:(group + 1) * group_width],
                          out_weight[group * group_width:(group + 1) * group_width],
                          preferred_element_type=jnp.float32)
        total = total + settle(product)
    student = total.astype(jnp.bfloat16)
    residue = (student.astype(jnp.float32) - teacher.astype(jnp.float32)).astype(jnp.bfloat16)
    grad_attended = jnp.dot(residue, out_weight.T, preferred_element_type=jnp.float32).astype(jnp.bfloat16)
    grad_blocks = heads_first(grad_attended)
    head_rows = jnp.arange(HEADS, dtype=jnp.int32)[:, None]

    def backward_tile(carry, tile_index):
        key_sum, value_sum = carry
        query_tile, key_tiles, value_tiles, listed_ids, live_slots, probs_low, attended_tile = forward_tile(tile_index)
        grad_tile = grad_blocks[:, tile_index].astype(jnp.float32)
        delta = jnp.sum(grad_tile * attended_tile.astype(jnp.float32), axis=2)
        dprob = jnp.einsum("hqd,hnkd->hqnk", grad_tile, value_tiles)
        dscore = settle(probs_low * (dprob - delta[:, :, None, None]))
        grad_query = (jnp.einsum("hqnk,hnkd->hqd", dscore, key_tiles) * score_scale).astype(jnp.bfloat16)
        key_part = settle(jnp.einsum("hqnk,hqd->hnkd", dscore, query_tile) * score_scale)
        value_part = settle(jnp.einsum("hqnk,hqd->hnkd", probs_low, grad_tile))
        target = jnp.where(live_slots, listed_ids, TILES).astype(jnp.int32)
        key_sum = key_sum.at[head_rows, target].add(key_part)
        value_sum = value_sum.at[head_rows, target].add(value_part)
        return (key_sum, value_sum), grad_query

    empty = jnp.zeros((HEADS, TILES + 1, TILE, HD), jnp.float32)
    (key_sum, value_sum), grad_stack = lax.scan(backward_tile, (empty, empty), tile_order)
    grad_queries = mapped_to_tokens(grad_stack)
    grad_keys = carry_to_tokens(key_sum[:, :TILES]).astype(jnp.bfloat16)
    grad_values = carry_to_tokens(value_sum[:, :TILES]).astype(jnp.bfloat16)
    return student, grad_queries, grad_keys, grad_values
```

```python
import jax
import jax.numpy as jnp
from jax import lax
from jax.experimental import pallas as pl
from jax.experimental.pallas import tpu as pltpu
from jax.sharding import Mesh, PartitionSpec as P

HD = 128
TW = 8
TILE = 256
SLOTS = 18
MASKED = -1e30
SCORE_SCALE = HD ** (-0.5)
LOG2_E = 1.4426950408889634

TILE_AXES = ("xf", "xr", "zr", "zc")
HEAD_AXES = ("y", "core")


def contract_last(left, right):
    return lax.dot_general(left, right, (((1,), (1,)), ((), ())), preferred_element_type=jnp.float32)


def contract_first(left, right):
    return lax.dot_general(left, right, (((0,), (0,)), ((), ())), preferred_element_type=jnp.float32)


def contract_inner(left, right):
    return lax.dot_general(left, right, (((1,), (0,)), ((), ())), preferred_element_type=jnp.float32)


def slot_refs(refs):
    return [(ref, index) for ref in refs for index in range(ref.shape[0])]


def forward_kernel(q_ref, bias_ref, *refs):
    windows, (weights_ref, attended_ref, inverse_ref, scores_ref) = refs[:6], refs[6:]
    slots = slot_refs(windows)
    for f in range(2):
        cols = slice(f * TILE, (f + 1) * TILE)
        query = q_ref[cols, :]
        highest = jnp.full((8, TILE), -jnp.inf, jnp.float32)
        for s, (ref, index) in enumerate(slots):
            scores = contract_last(ref[index, 0], query) * (SCORE_SCALE * LOG2_E)
            scores = scores + bias_ref[s : s + 1, cols]
            scores_ref[s] = scores
            highest = jnp.maximum(highest, jnp.max(scores.reshape(TILE // 8, 8, TILE), axis=0))
        highest = jnp.max(highest, axis=0, keepdims=True)
        total = jnp.zeros((8, TILE), jnp.float32)
        summed = jnp.zeros((HD, TILE), jnp.float32)
        for s, (ref, index) in enumerate(slots):
            weights = jnp.exp2(scores_ref[s] - highest)
            total = total + jnp.sum(weights.reshape(TILE // 8, 8, TILE), axis=0)
            weights = weights.astype(jnp.bfloat16)
            weights_ref[s, :, cols] = weights
            summed = summed + contract_first(ref[index, 1], weights)
        inverse = 1.0 / jnp.sum(total, axis=0, keepdims=True)
        inverse_ref[:, cols] = jnp.broadcast_to(inverse, (8, TILE))
        attended_ref[cols, :] = (summed * inverse).T.astype(jnp.bfloat16)


def backward_kernel(q_ref, grad_ref, attended_ref, inverse_ref, weights_ref, *refs):
    windows, (grad_q_ref, *parts) = refs[:6], refs[6:]
    slots = slot_refs(windows)
    outs = slot_refs(parts)
    queries = [q_ref[f * TILE : (f + 1) * TILE, :] for f in range(2)]
    grads = [grad_ref[f * TILE : (f + 1) * TILE, :] for f in range(2)]
    deltas = []
    for f in range(2):
        product = grads[f].astype(jnp.float32) * attended_ref[f * TILE : (f + 1) * TILE, :].astype(jnp.float32)
        deltas.append(jnp.sum(product.T, axis=0, keepdims=True))
    grad_q = [jnp.zeros((HD, TILE), jnp.float32) for _ in range(2)]
    for s, ((ref, index), (out, out_index)) in enumerate(zip(slots, outs)):
        key, value = ref[index, 0], ref[index, 1]
        grad_key = jnp.zeros((TILE, HD), jnp.float32)
        grad_value = jnp.zeros((TILE, HD), jnp.float32)
        for f in range(2):
            cols = slice(f * TILE, (f + 1) * TILE)
            dprob = contract_last(value, grads[f])
            probs = weights_ref[s, :, cols].astype(jnp.float32) * inverse_ref[0:1, cols]
            dscore = (probs * (dprob - deltas[f])).astype(jnp.bfloat16)
            grad_key = grad_key + contract_inner(dscore, queries[f])
            grad_value = grad_value + contract_inner(probs.astype(jnp.bfloat16), grads[f])
            grad_q[f] = grad_q[f] + contract_first(key, dscore)
        out[out_index, 0] = (grad_key * SCORE_SCALE).astype(jnp.bfloat16)
        out[out_index, 1] = grad_value.astype(jnp.bfloat16)
    for f in range(2):
        grad_q_ref[f * TILE : (f + 1) * TILE, :] = (grad_q[f] * SCORE_SCALE).T.astype(jnp.bfloat16)


def project_kernel(group_ref, attended_ref, weight_ref, teacher_ref, student_ref, grad_ref, total_ref):
    step = pl.program_id(0)
    group = group_ref[0]
    acc = jnp.zeros((TILE, TILE), jnp.float32)
    for g in range(8):
        rows = jnp.concatenate([attended_ref[0, g], attended_ref[1, g]], axis=1)
        acc = acc + contract_inner(rows, weight_ref[g])
    student = acc.astype(jnp.bfloat16)

    @pl.when(step == group)
    def _():
        student_ref[...] = student

    residue = (student.astype(jnp.float32) - teacher_ref[0].astype(jnp.float32)).astype(jnp.bfloat16)
    update = contract_last(residue, weight_ref[group])

    @pl.when(step == 0)
    def _():
        total_ref[...] = update

    @pl.when(step > 0)
    def _():
        total_ref[...] += update

    @pl.when(step == 7)
    def _():
        grad_ref[...] = total_ref[...].astype(jnp.bfloat16)


def vmem_specs(count):
    return [pl.BlockSpec(memory_space=pltpu.VMEM) for _ in range(count)]


def forward(query, bias, windows):
    return pl.pallas_call(
        forward_kernel,
        out_shape=(
            jax.ShapeDtypeStruct((SLOTS, TILE, 2 * TILE), jnp.bfloat16),
            jax.ShapeDtypeStruct((2 * TILE, HD), jnp.bfloat16),
            jax.ShapeDtypeStruct((8, 2 * TILE), jnp.float32),
        ),
        in_specs=vmem_specs(2 + len(windows)),
        out_specs=tuple(vmem_specs(3)),
        scratch_shapes=[pltpu.VMEM((SLOTS, TILE, TILE), jnp.float32)],
        compiler_params=pltpu.CompilerParams(vmem_limit_bytes=48 * 1024 * 1024),
        cost_estimate=pl.CostEstimate(flops=3_000_000_000, bytes_accessed=8_000_000, transcendentals=2_400_000),
        name="attend",
    )(query, bias, *windows)


def backward(query, grad, attended, inverse, weights, windows):
    out_shape = [jax.ShapeDtypeStruct((2 * TILE, HD), jnp.bfloat16)]
    out_shape += [jax.ShapeDtypeStruct(window.shape, jnp.bfloat16) for window in windows]
    return pl.pallas_call(
        backward_kernel,
        out_shape=tuple(out_shape),
        in_specs=vmem_specs(5 + len(windows)),
        out_specs=tuple(vmem_specs(len(out_shape))),
        compiler_params=pltpu.CompilerParams(vmem_limit_bytes=48 * 1024 * 1024),
        cost_estimate=pl.CostEstimate(flops=6_000_000_000, bytes_accessed=10_000_000, transcendentals=0),
        name="attend_back",
    )(query, grad, attended, inverse, weights, *windows)


def project(group, attended, weight, teacher):
    width = TILE
    return pl.pallas_call(
        project_kernel,
        grid_spec=pltpu.PrefetchScalarGridSpec(
            num_scalar_prefetch=1,
            grid=(8,),
            in_specs=[
                pl.BlockSpec((2, 8, TILE, HD), lambda j, g: (0, 0, 0, 0)),
                pl.BlockSpec((8, TILE, width), lambda j, g: (0, 0, j)),
                pl.BlockSpec((1, TILE, TILE), lambda j, g: (j, 0, 0)),
            ],
            out_specs=[
                pl.BlockSpec((TILE, TILE), lambda j, g: (0, 0)),
                pl.BlockSpec((TILE, TILE), lambda j, g: (0, 0)),
            ],
            scratch_shapes=[pltpu.VMEM((TILE, TILE), jnp.float32)],
        ),
        out_shape=[jax.ShapeDtypeStruct((TILE, TILE), jnp.bfloat16)] * 2,
        compiler_params=pltpu.CompilerParams(vmem_limit_bytes=48 * 1024 * 1024),
        cost_estimate=pl.CostEstimate(flops=2_500_000_000, bytes_accessed=10_000_000, transcendentals=0),
        name="project",
    )(group, attended, weight, teacher)


def column_shift(value, step, lines):
    pairs = [
        (line * TW + col, line * TW + col + step)
        for line in lines
        for col in range(TW)
        if 0 <= col + step < TW
    ]
    return lax.ppermute(value, ("xr", "zr", "zc"), pairs)


ALL_LINES = (0, 1, 2, 3)
MIDDLE_LINES = (1, 2)


def slot_tiles(xr, zr, zc):
    third = 2 - xr
    middle = xr != zr
    tiles = []
    for step in (0, -1, 1):
        col = zc + step
        inside = (col >= 0) & (col < TW)
        for f in range(2):
            for pair_row in range(2):
                tiles.append(jnp.where(inside, f * 32 + (2 * xr + pair_row) * TW + col, -2))
    for step in (0, -1, 1):
        col = zc + step
        inside = (col >= 0) & (col < TW) & middle
        for f in range(2):
            tiles.append(jnp.where(inside, f * 32 + third * TW + col, -2))
    return jnp.stack(tiles)


def body(queries, keys, values, out_weight, teacher, block_lists):
    xf, xr, zr, zc = (lax.axis_index(axis) for axis in TILE_AXES)
    group = lax.axis_index(HEAD_AXES)
    swap = [(0, 1), (1, 0)]

    listed = jnp.any(block_lists[:, 0, :, None] == slot_tiles(xr, zr, zc)[None, None, :], axis=1)
    listed = jnp.pad(listed.astype(jnp.bfloat16), ((0, 0), (0, HD - SLOTS)))
    query_heads = queries.reshape(TILE, 2, HD).transpose(1, 0, 2)
    with_mask = jnp.concatenate(
        [query_heads, jnp.broadcast_to(listed[:, None, :], (2, 16, HD))], axis=1
    )
    mine = lax.dynamic_index_in_dim(with_mask, xf, 0, keepdims=False)
    others = lax.dynamic_index_in_dim(with_mask, 1 - xf, 0, keepdims=False)

    heads = jnp.stack([keys.reshape(TILE, 2, HD), values.reshape(TILE, 2, HD)])
    heads = heads.transpose(2, 0, 1, 3)
    send = jnp.broadcast_to(heads[:, None], (2, 2, 2, TILE, HD)).reshape(4, 2, TILE, HD)
    rows = lax.all_to_all(send, ("xf", "zr"), 0, 0, tiled=True)

    got = lax.ppermute(others, "xf", swap)
    pair = jnp.where(xf == 0, jnp.stack([mine, got]), jnp.stack([got, mine]))
    query = pair[:, :TILE].reshape(2 * TILE, HD)
    allowed = pair[:, TILE, :SLOTS].T
    bias = jnp.where(jnp.repeat(allowed, TILE, axis=1) > 0.5, 0.0, MASKED).astype(jnp.float32)

    packed = jnp.concatenate([out_weight, teacher.reshape(32, 2048)])
    packed = lax.all_gather(packed, HEAD_AXES)

    third_send = jnp.where(zr == 0, rows.reshape(2, 2, 2, TILE, HD)[:, 1], rows.reshape(2, 2, 2, TILE, HD)[:, 0])
    third = lax.ppermute(third_send, ("xr", "zr"), [(0, 2), (3, 1)])
    rows_left = column_shift(rows, 1, ALL_LINES)
    rows_right = column_shift(rows, -1, ALL_LINES)
    third_left = column_shift(third, 1, MIDDLE_LINES)
    third_right = column_shift(third, -1, MIDDLE_LINES)
    windows = (rows, rows_left, rows_right, third, third_left, third_right)

    weights, attended, inverse = forward(query, bias, windows)

    spread = jnp.broadcast_to(attended.reshape(2, 1, TILE, HD), (2, 8, TILE, HD)).reshape(16, TILE, HD)
    gathered = lax.all_to_all(spread, ("xf",) + HEAD_AXES, 0, 0, tiled=True).reshape(2, 8, TILE, HD)
    teacher_all = packed[:, TILE:, :].reshape(8, TILE, TILE)
    student, grad_own = project(group.astype(jnp.int32)[None], gathered, packed, teacher_all)

    grad_heads = grad_own.reshape(TILE, 2, HD).transpose(1, 0, 2)
    grad_mine = lax.dynamic_index_in_dim(grad_heads, xf, 0, keepdims=False)
    grad_got = lax.ppermute(lax.dynamic_index_in_dim(grad_heads, 1 - xf, 0, keepdims=False), "xf", swap)
    grad = jnp.where(
        xf == 0, jnp.concatenate([grad_mine, grad_got]), jnp.concatenate([grad_got, grad_mine])
    )

    grad_query, part, part_left, part_right, far, far_left, far_right = backward(
        query, grad, attended, inverse, weights, windows
    )

    def sum_of(*terms):
        total = terms[0].astype(jnp.float32)
        for term in terms[1:]:
            total = total + term.astype(jnp.float32)
        return total

    far_from_right = column_shift(far_left, -1, MIDDLE_LINES)
    far_from_left = column_shift(far_right, 1, MIDDLE_LINES)
    part_from_right = column_shift(part_left, -1, ALL_LINES)
    part_from_left = column_shift(part_right, 1, ALL_LINES)
    far_sum = sum_of(far, far_from_right, far_from_left).astype(jnp.bfloat16)
    third_back = lax.ppermute(far_sum, ("xr", "zr"), [(2, 0), (1, 3)])
    row_of_third = jnp.arange(2) == 1 - zr
    third_back = jnp.where(row_of_third[None, :, None, None, None], third_back[:, None], 0)
    part_sum = sum_of(part, part_from_right, part_from_left, third_back.reshape(4, 2, TILE, HD))
    back = lax.all_to_all(part_sum.astype(jnp.bfloat16), ("xf", "zr"), 0, 0, tiled=True)
    back = back.reshape(2, 2, 2, TILE, HD).astype(jnp.float32)
    back = (back[:, 0] + back[:, 1]).astype(jnp.bfloat16)
    back = back.transpose(1, 2, 0, 3).reshape(2, TILE, 2 * HD)

    own_q = lax.dynamic_slice_in_dim(grad_query, xf * TILE, TILE)
    got_q = lax.ppermute(lax.dynamic_slice_in_dim(grad_query, (1 - xf) * TILE, TILE), "xf", swap)
    grad_queries = jnp.where(
        xf == 0, jnp.concatenate([own_q, got_q], axis=1), jnp.concatenate([got_q, own_q], axis=1)
    )
    return student, grad_queries, back[0], back[1]


def solution(mesh):
    split = Mesh(mesh.devices.reshape(2, 2, 2, 8, 4, 2), TILE_AXES + HEAD_AXES)
    both = P(TILE_AXES, HEAD_AXES)
    return jax.shard_map(
        body,
        mesh=split,
        in_specs=(both, both, both, P(HEAD_AXES, None), both, P(HEAD_AXES, TILE_AXES, None)),
        out_specs=(both, both, both, both),
        check_vma=False,
    )
```

```python
import functools

import jax
import jax.numpy as jnp
from jax import lax
from jax.experimental import pallas as pl
from jax.experimental.pallas import tpu as pltpu
from jax.sharding import Mesh, PartitionSpec as P

HD = 128
TW = 8
TILE = 256
SLOTS = 18
MASKED = -1e30
SCORE_SCALE = HD ** (-0.5)
LOG2_E = 1.4426950408889634

TILE_AXES = ("xf", "xr", "zr", "zc")
HEAD_AXES = ("y", "core")


def contract_last(left, right):
    return lax.dot_general(left, right, (((1,), (1,)), ((), ())), preferred_element_type=jnp.float32)


def contract_first(left, right):
    return lax.dot_general(left, right, (((0,), (0,)), ((), ())), preferred_element_type=jnp.float32)


def contract_inner(left, right):
    return lax.dot_general(left, right, (((1,), (0,)), ((), ())), preferred_element_type=jnp.float32)


def slot_refs(refs):
    return [(ref, index) for ref in refs for index in range(ref.shape[0])]


def copy_all(pairs, sems):
    copies = [pltpu.make_async_copy(source, target, sems.at[i]) for i, (source, target) in enumerate(pairs)]
    for copy in copies:
        copy.start()
    return copies


def prepare_kernel(
    place_ref, queries_ref, keys_ref, values_ref, mine_ref, other_ref, q_mine_ref, q_other_ref, in_ref, sems
):
    sources = (keys_ref, values_ref, queries_ref)
    copies = copy_all([(source, in_ref.at[i]) for i, source in enumerate(sources)], sems)
    first = pl.multiple_of(place_ref[0] * HD, HD)
    mine, other = pl.ds(first, HD), pl.ds(pl.multiple_of(HD - first, HD), HD)
    for index in range(2):
        copies[index].wait()
        mine_ref[index] = in_ref[index, :, mine]
        other_ref[index] = in_ref[index, :, other]
    copies[2].wait()
    q_mine_ref[...] = in_ref[2, :, mine]
    q_other_ref[...] = in_ref[2, :, other]


def prepare(place, queries, keys, values):
    out_shape = [shape(2, TILE, HD)] * 2 + [shape(TILE, HD)] * 2
    return pl.pallas_call(
        prepare_kernel,
        out_shape=tuple(out_shape),
        in_specs=place_spec() + [pl.BlockSpec(memory_space=pltpu.HBM)] * 3,
        out_specs=tuple(vmem_specs(len(out_shape))),
        scratch_shapes=[pltpu.VMEM((3, TILE, TILE), jnp.bfloat16), pltpu.SemaphoreType.DMA((3,))],
        compiler_params=pltpu.CompilerParams(vmem_limit_bytes=8 * 1024 * 1024),
        cost_estimate=pl.CostEstimate(flops=1_000_000, bytes_accessed=2_000_000, transcendentals=0),
        name="prepare",
    )(place, queries, keys, values)


def pair_kernel(mine_ref, frame_ref, pair_ref):
    pair_ref[0] = mine_ref[...]
    for part in range(2):
        pair_ref[1, part] = frame_ref[part * TILE : (part + 1) * TILE, :]


def forward_kernel(allowed_ref, q_mine_ref, frame_ref, *refs):
    windows, kept_refs, refs = refs[:9], refs[9:12], refs[12:]
    attended_refs, (inverse_ref, window_ref, scores_ref, weights_ref, sems, in_sems) = refs[:2], refs[2:]
    pairs, start = [], 0
    for window in windows:
        pairs.append((window, window_ref.at[pl.ds(start, window.shape[0])]))
        start += window.shape[0]
    arriving = dict(zip(range(0, SLOTS, 2), copy_all(pairs, in_sems)))
    copies = []

    def bias_of(f, s):
        return jnp.where(allowed_ref[f, s] > 0, 0.0, MASKED)

    for f in range(2):
        cols = slice(f * TILE, (f + 1) * TILE)
        query = q_mine_ref[...] if f == 0 else frame_ref[2 * TILE : 3 * TILE, :]
        highest = jnp.full((8, TILE), -jnp.inf, jnp.float32)
        for s in range(SLOTS):
            if f == 0 and s in arriving:
                arriving[s].wait()
            products = contract_last(window_ref[s, 0], query)
            scores_ref[s] = products
            top = jnp.max(products.reshape(TILE // 8, 8, TILE), axis=0) * (SCORE_SCALE * LOG2_E)
            highest = jnp.maximum(highest, top + bias_of(f, s))
        highest = jnp.max(highest, axis=0, keepdims=True)
        total = jnp.zeros((8, TILE), jnp.float32)
        summed = jnp.zeros((HD, TILE), jnp.float32)
        for s in range(SLOTS):
            weights = jnp.exp2(scores_ref[s] * (SCORE_SCALE * LOG2_E) + (bias_of(f, s) - highest))
            total = total + jnp.sum(weights.reshape(TILE // 8, 8, TILE), axis=0)
            weights = weights.astype(jnp.bfloat16)
            weights_ref[f, s] = weights
            summed = summed + contract_first(window_ref[s, 1], weights)
        inverse = 1.0 / jnp.sum(total, axis=0, keepdims=True)
        inverse_ref[:, cols] = jnp.broadcast_to(inverse, (8, TILE))
        attended_refs[f][...] = (summed * inverse).T.astype(jnp.bfloat16)
        start = 0
        for part, kept_ref in enumerate(kept_refs):
            count = kept_ref.shape[1]
            copy = pltpu.make_async_copy(
                weights_ref.at[f, pl.ds(start, count)], kept_ref.at[f], sems.at[f, part]
            )
            copy.start()
            copies.append(copy)
            start += count
    for copy in copies:
        copy.wait()


def backward_kernel(
    count, last, q_mine_ref, frame_ref, grad_mine_ref, grad_got_ref, own_ref, other_ref, inverse_ref, *refs
):
    before_ref, kept_ref, *refs = refs
    windows, (grad_q_ref, *parts) = refs[:count], refs[count : 2 * count + 1]
    weights_ref, sems, *window_refs = refs[2 * count + 1 :]
    copies = copy_all([(kept_ref, weights_ref), *zip(windows, window_refs)], sems)
    queries = [q_mine_ref[...], frame_ref[2 * TILE : 3 * TILE, :]]
    grads = [grad_mine_ref[...], grad_got_ref[...]]
    deltas = []
    for f in range(2):
        product = grads[f].astype(jnp.float32) * (own_ref, other_ref)[f][...].astype(jnp.float32)
        deltas.append(jnp.sum(product.T, axis=0, keepdims=True))
    grad_q = [before_ref[f] for f in range(2)]
    for copy in copies:
        copy.wait()
    for s, ((ref, index), (out, out_index)) in enumerate(zip(slot_refs(window_refs), slot_refs(parts))):
        key, value = ref[index, 0], ref[index, 1]
        grad_key = jnp.zeros((TILE, HD), jnp.float32)
        grad_value = jnp.zeros((TILE, HD), jnp.float32)
        for f in range(2):
            cols = slice(f * TILE, (f + 1) * TILE)
            dprob = contract_last(value, grads[f])
            probs = weights_ref[f, s].astype(jnp.float32) * inverse_ref[0:1, cols]
            dscore = (probs * (dprob - deltas[f])).astype(jnp.bfloat16)
            grad_key = grad_key + contract_inner(dscore, queries[f])
            grad_value = grad_value + contract_inner(probs.astype(jnp.bfloat16), grads[f])
            grad_q[f] = grad_q[f] + contract_first(key, dscore)
        out[out_index, 0] = (grad_key * SCORE_SCALE).astype(jnp.bfloat16)
        out[out_index, 1] = grad_value.astype(jnp.bfloat16)
    for f in range(2):
        if last:
            grad_q_ref[f] = (grad_q[f] * SCORE_SCALE).T.astype(jnp.bfloat16)
        else:
            grad_q_ref[f] = grad_q[f]


def project_kernel(*refs):
    attended_refs, pack_refs, out_ref = refs[:4], refs[4:8], refs[8]
    for block in range(8):
        cols = slice(block * TILE, (block + 1) * TILE)
        total = jnp.zeros((TILE, TILE), jnp.float32)
        for attended_ref, pack_ref in zip(attended_refs, pack_refs):
            total = total + contract_inner(attended_ref[...], pack_ref[:, cols])
        out_ref[:, cols] = total.astype(jnp.bfloat16)


def residue_kernel(place_ref, mine_ref, other_ref, weight_ref, *refs):
    teacher_refs, (student_ref, mine_grad_ref, other_grad_ref) = refs[:4], refs[4:]
    row, core = place_ref[1], place_ref[2]
    grad = jnp.zeros((TILE, TILE), jnp.float32)
    for side in range(2):
        for back in range(4):
            group = lax.rem(row + 4 - back, 4) * 2 + (core if side == 0 else 1 - core)
            cols = pl.ds(pl.multiple_of(group * TILE, TILE), TILE)
            student = mine_ref[:, cols].astype(jnp.float32) + other_ref[:, cols].astype(jnp.float32)
            student = student.astype(jnp.bfloat16)
            if side == 0 and back == 0:
                student_ref[...] = student
            teacher = teacher_refs[back][:, side * TILE : (side + 1) * TILE]
            residue = (student.astype(jnp.float32) - teacher.astype(jnp.float32)).astype(jnp.bfloat16)
            grad = grad + contract_last(residue, weight_ref[:, cols])
    mine_grad_ref[...] = grad[:, :HD].astype(jnp.bfloat16)
    other_grad_ref[...] = grad[:, HD:].astype(jnp.bfloat16)


def merge_kernel(part_ref, right_ref, left_ref, third_ref, out_ref):
    out_ref[...] = sum_of(part_ref[...], right_ref[...], left_ref[...], third_ref[...]).astype(jnp.bfloat16)


def far_kernel(part_ref, right_ref, left_ref, out_ref):
    out_ref[...] = sum_of(part_ref[...], right_ref[...], left_ref[...]).astype(jnp.bfloat16)


def frame_kernel(part_ref, right_ref, left_ref, row_ref, grad_q_ref, frame_ref):
    total = sum_of(part_ref[1], right_ref[1], left_ref[1], row_ref[1]).astype(jnp.bfloat16)
    frame_ref[0] = total[0]
    frame_ref[1] = total[1]
    frame_ref[2] = grad_q_ref[1]


def join_kernel(place_ref, part_ref, right_ref, left_ref, row_ref, grad_q_ref, frame_ref, *outs):
    first = pl.multiple_of(place_ref[0] * HD, HD)
    mine, other = pl.ds(first, HD), pl.ds(pl.multiple_of(HD - first, HD), HD)
    own = sum_of(part_ref[0], right_ref[0], left_ref[0], row_ref[0]).astype(jnp.bfloat16)
    outs[0][:, mine] = grad_q_ref[0]
    outs[0][:, other] = frame_ref[2]
    for index in range(2):
        outs[1 + index][:, mine] = own[index]
        outs[1 + index][:, other] = frame_ref[index]


def vmem_specs(count):
    return [pl.BlockSpec(memory_space=pltpu.VMEM) for _ in range(count)]


def any_specs(count):
    return [pl.BlockSpec(memory_space=pl.ANY) for _ in range(count)]


def place_spec():
    return [pl.BlockSpec(memory_space=pltpu.SMEM)]


def shape(*dims, dtype=jnp.bfloat16):
    return jax.ShapeDtypeStruct(dims, dtype)


def simple(kernel, name, out_shape, *args, place=None, limit=8):
    head = [] if place is None else [place]
    return pl.pallas_call(
        kernel,
        out_shape=tuple(out_shape),
        in_specs=place_spec() * len(head) + vmem_specs(len(args)),
        out_specs=tuple(vmem_specs(len(out_shape))),
        compiler_params=pltpu.CompilerParams(vmem_limit_bytes=limit * 1024 * 1024),
        cost_estimate=pl.CostEstimate(flops=1_000_000, bytes_accessed=2_000_000, transcendentals=0),
        name=name,
    )(*head, *args)


def forward(allowed, q_mine, frame, windows):
    kept = [shape(2, 6, TILE, TILE) for _ in range(3)]
    return pl.pallas_call(
        forward_kernel,
        out_shape=(*kept, shape(TILE, HD), shape(TILE, HD), shape(8, 2 * TILE, dtype=jnp.float32)),
        in_specs=place_spec() + vmem_specs(2) + any_specs(len(windows)),
        out_specs=tuple(any_specs(3) + vmem_specs(3)),
        scratch_shapes=[
            pltpu.VMEM((SLOTS, 2, TILE, HD), jnp.bfloat16),
            pltpu.VMEM((SLOTS, TILE, TILE), jnp.float32),
            pltpu.VMEM((2, SLOTS, TILE, TILE), jnp.bfloat16),
            pltpu.SemaphoreType.DMA((2, 3)),
            pltpu.SemaphoreType.DMA((9,)),
        ],
        compiler_params=pltpu.CompilerParams(vmem_limit_bytes=18 * 1024 * 1024),
        cost_estimate=pl.CostEstimate(flops=3_000_000_000, bytes_accessed=8_000_000, transcendentals=2_400_000),
        name="attend",
    )(allowed, q_mine, frame, *windows)


def backward(common, before, weights, windows, last=False):
    if last:
        out_shape = [shape(2, TILE, HD)]
    else:
        out_shape = [shape(2, HD, TILE, dtype=jnp.float32)]
    out_shape += [shape(*window.shape) for window in windows]
    blocks = 2 * weights.shape[1]
    return pl.pallas_call(
        functools.partial(backward_kernel, len(windows), last),
        out_shape=tuple(out_shape),
        in_specs=vmem_specs(len(common) + 1) + any_specs(1 + len(windows)),
        out_specs=tuple(vmem_specs(len(out_shape))),
        scratch_shapes=[
            pltpu.VMEM(weights.shape, jnp.bfloat16),
            pltpu.SemaphoreType.DMA((1 + len(windows),)),
            *[pltpu.VMEM(window.shape, jnp.bfloat16) for window in windows],
        ],
        compiler_params=pltpu.CompilerParams(vmem_limit_bytes=10 * 1024 * 1024),
        cost_estimate=pl.CostEstimate(
            flops=blocks * 8 * TILE * TILE * HD, bytes_accessed=blocks * 300_000, transcendentals=0
        ),
        name="attend_back",
    )(*common, before, weights, *windows)


def project(attended, packs):
    return pl.pallas_call(
        project_kernel,
        in_specs=vmem_specs(8),
        out_specs=pl.BlockSpec(memory_space=pltpu.VMEM),
        out_shape=jax.ShapeDtypeStruct((TILE, 8 * TILE), jnp.bfloat16),
        compiler_params=pltpu.CompilerParams(vmem_limit_bytes=10 * 1024 * 1024),
        cost_estimate=pl.CostEstimate(flops=1_100_000_000, bytes_accessed=6_000_000, transcendentals=0),
        name="project",
    )(*attended, *packs)


def residue_grad(place, mine, other, packs):
    out_shape = [shape(TILE, TILE), shape(TILE, HD), shape(TILE, HD)]
    return pl.pallas_call(
        residue_kernel,
        grid=(1,),
        out_shape=tuple(out_shape),
        in_specs=place_spec()
        + vmem_specs(2)
        + [pl.BlockSpec((TILE, 8 * TILE), lambda i: (0, 0))]
        + [pl.BlockSpec((TILE, 2 * TILE), lambda i: (0, 4)) for _ in packs],
        out_specs=tuple(vmem_specs(len(out_shape))),
        compiler_params=pltpu.CompilerParams(vmem_limit_bytes=10 * 1024 * 1024),
        cost_estimate=pl.CostEstimate(flops=300_000_000, bytes_accessed=5_000_000, transcendentals=0),
        name="residue",
    )(place, mine, other, packs[0], *packs)


def column_shift(value, step, lines):
    pairs = [
        (line * TW + col, line * TW + col + step)
        for line in lines
        for col in range(TW)
        if 0 <= col + step < TW
    ]
    return lax.ppermute(value, ("xr", "zr", "zc"), pairs)


ALL_LINES = (0, 1, 2, 3)
MIDDLE_LINES = (1, 2)
SWAP = [(0, 1), (1, 0)]


def slot_tiles(frame, xr, zr, zc):
    tiles = []
    for row, live in ((2 * xr + zr, True), (2 * xr + 1 - zr, True), (2 - xr, xr != zr)):
        for step in (0, -1, 1):
            col = zc + step
            inside = (col >= 0) & (col < TW) & live
            for f in (frame, 1 - frame):
                tiles.append(jnp.where(inside, f * 32 + row * TW + col, -2))
    return jnp.stack(tiles)


def beside(value, lines):
    return column_shift(value, 1, lines), column_shift(value, -1, lines)


def from_rows(value):
    return [lax.ppermute(value, "y", [(i, (i + step) % 4) for i in range(4)]) for step in (1, 2, 3)]


def sum_of(*terms):
    total = terms[0].astype(jnp.float32)
    for term in terms[1:]:
        total = total + term.astype(jnp.float32)
    return total


def body(queries, keys, values, out_weight, teacher, block_lists):
    xf, xr, zr, zc = (lax.axis_index(axis) for axis in TILE_AXES)
    place = jnp.stack([xf, lax.axis_index("y"), lax.axis_index("core")]).astype(jnp.int32)

    kv_mine, kv_other, q_mine, q_other = prepare(place, queries, keys, values)

    def listed(head, frame):
        lists = lax.dynamic_index_in_dim(block_lists[:, 0], head, 0, keepdims=False)
        return jnp.any(lists[:, None] == slot_tiles(frame, xr, zr, zc)[None, :], axis=0)

    mask_row = jnp.pad(listed(1 - xf, 1 - xf).astype(jnp.bfloat16), (0, HD - SLOTS))
    message = jnp.concatenate(
        [kv_other.reshape(2 * TILE, HD), q_other, jnp.broadcast_to(mask_row[None], (16, HD))]
    )
    xf_got = lax.ppermute(message, "xf", SWAP)
    allowed = jnp.stack([listed(xf, xf), xf_got[3 * TILE, :SLOTS] > 0.5]).astype(jnp.int32)

    pair = simple(pair_kernel, "pair", [shape(2, 2, TILE, HD)], kv_mine, xf_got)[0]
    row = lax.ppermute(pair, "zr", SWAP)
    third = lax.ppermute(row, ("xr", "zr"), [(0, 2), (3, 1)])
    own_windows = (pair, *beside(pair, ALL_LINES))
    row_windows = (row, *beside(row, ALL_LINES))
    third_windows = (third, *beside(third, MIDDLE_LINES))

    weight_heads = out_weight.reshape(2, HD, 8 * TILE)
    first_head = jnp.where(xf == 0, weight_heads[0], weight_heads[1])
    second_head = jnp.where(xf == 0, weight_heads[1], weight_heads[0])
    far_teacher = lax.ppermute(teacher, "core", SWAP)
    first_head, _ = lax.optimization_barrier((first_head, xf_got))
    pack = jnp.concatenate([jnp.concatenate([first_head, second_head]), teacher, far_teacher], axis=1)
    ring = [(i, (i + 1) % 4) for i in range(4)]
    up = lax.ppermute(pack, "y", ring)
    down = lax.ppermute(pack, "y", [(i, (i + 3) % 4) for i in range(4)])
    across = lax.ppermute(up, "y", ring)
    packs = [pack, up, across, down]

    *weights, own, other, inverse = forward(
        allowed, q_mine, xf_got, own_windows + row_windows + third_windows
    )

    got = lax.ppermute(other, "xf", SWAP)
    attended = jnp.concatenate([own, got], axis=1)
    partial_mine = project([attended] + from_rows(attended), packs)
    partial_other = lax.ppermute(partial_mine, "core", SWAP)
    student, grad_mine, grad_other = residue_grad(place, partial_mine, partial_other, packs)
    grad_got = lax.ppermute(grad_other, "xf", SWAP)

    own_weights, row_weights, third_weights = weights
    common = (q_mine, xf_got, grad_mine, grad_got, own, other, inverse)
    before = jnp.zeros((2, HD, TILE), jnp.float32)
    before, far, far_left, far_right = backward(common, before, third_weights, third_windows)
    before, part, part_left, part_right = backward(common, before, row_weights, row_windows)
    grad_query, near, near_left, near_right = backward(common, before, own_weights, own_windows, last=True)

    def returned(left, right, lines):
        return column_shift(left, -1, lines), column_shift(right, 1, lines)

    far_sum = simple(
        far_kernel, "far_sum", [shape(2, 2, TILE, HD)], far, *returned(far_left, far_right, MIDDLE_LINES)
    )[0]
    third_back = lax.ppermute(far_sum, ("xr", "zr"), [(2, 0), (1, 3)])
    row_sum = simple(
        merge_kernel,
        "merge",
        [shape(2, 2, TILE, HD)],
        part,
        *returned(part_left, part_right, ALL_LINES),
        third_back,
    )[0]
    row_back = lax.ppermute(row_sum, "zr", SWAP)
    from_right, from_left = returned(near_left, near_right, ALL_LINES)
    sums = (near, from_right, from_left, row_back, grad_query)
    frame_sum = simple(frame_kernel, "frame_sum", [shape(3, TILE, HD)], *sums)[0]
    xf_back = lax.ppermute(frame_sum, "xf", SWAP)
    grad_queries, grad_keys, grad_values = simple(
        join_kernel, "join", [shape(TILE, TILE)] * 3, *sums, xf_back, place=place
    )
    return student, grad_queries, grad_keys, grad_values


def solution(mesh):
    split = Mesh(mesh.devices.reshape(2, 2, 2, 8, 4, 2), TILE_AXES + HEAD_AXES)
    both = P(TILE_AXES, HEAD_AXES)
    return jax.shard_map(
        body,
        mesh=split,
        in_specs=(both, both, both, P(HEAD_AXES, None), both, P(HEAD_AXES, TILE_AXES, None)),
        out_specs=(both, both, both, both),
        check_vma=False,
    )
```

```python
import functools

import jax
import jax.numpy as jnp
from jax import lax
from jax.experimental import pallas as pl
from jax.experimental.pallas import tpu as pltpu
from jax.sharding import Mesh, PartitionSpec as P

HD = 128
TW = 8
TILE = 256
SLOTS = 18
MASKED = -1e30
SCORE_SCALE = HD ** (-0.5)
LOG2_E = 1.4426950408889634

TILE_AXES = ("xf", "xr", "zr", "zc")
HEAD_AXES = ("y", "core")


def contract_last(left, right):
    return lax.dot_general(left, right, (((1,), (1,)), ((), ())), preferred_element_type=jnp.float32)


def contract_first(left, right):
    return lax.dot_general(left, right, (((0,), (0,)), ((), ())), preferred_element_type=jnp.float32)


def contract_inner(left, right):
    return lax.dot_general(left, right, (((1,), (0,)), ((), ())), preferred_element_type=jnp.float32)


def slot_refs(refs):
    return [(ref, index) for ref in refs for index in range(ref.shape[0])]


def copy_all(pairs, sems):
    copies = [pltpu.make_async_copy(source, target, sems.at[i]) for i, (source, target) in enumerate(pairs)]
    for copy in copies:
        copy.start()
    return copies


def prepare_kernel(
    place_ref, queries_ref, keys_ref, values_ref, mine_ref, other_ref, q_mine_ref, q_other_ref, in_ref, sems
):
    sources = (keys_ref, values_ref, queries_ref)
    copies = copy_all([(source, in_ref.at[i]) for i, source in enumerate(sources)], sems)
    first = pl.multiple_of(place_ref[0] * HD, HD)
    mine, other = pl.ds(first, HD), pl.ds(pl.multiple_of(HD - first, HD), HD)
    for index in range(2):
        copies[index].wait()
        mine_ref[index] = in_ref[index, :, mine]
        other_ref[index] = in_ref[index, :, other]
    copies[2].wait()
    q_mine_ref[...] = in_ref[2, :, mine]
    q_other_ref[...] = in_ref[2, :, other]


def prepare(place, queries, keys, values):
    out_shape = [shape(2, TILE, HD)] * 2 + [shape(TILE, HD)] * 2
    return pl.pallas_call(
        prepare_kernel,
        out_shape=tuple(out_shape),
        in_specs=place_spec() + [pl.BlockSpec(memory_space=pltpu.HBM)] * 3,
        out_specs=tuple(vmem_specs(len(out_shape))),
        scratch_shapes=[pltpu.VMEM((3, TILE, TILE), jnp.bfloat16), pltpu.SemaphoreType.DMA((3,))],
        compiler_params=pltpu.CompilerParams(vmem_limit_bytes=8 * 1024 * 1024),
        cost_estimate=pl.CostEstimate(flops=1_000_000, bytes_accessed=2_000_000, transcendentals=0),
        name="prepare",
    )(place, queries, keys, values)


def pair_kernel(mine_ref, frame_ref, pair_ref):
    pair_ref[0] = mine_ref[...]
    for part in range(2):
        pair_ref[1, part] = frame_ref[part * TILE : (part + 1) * TILE, :]


def forward_kernel(allowed_ref, q_mine_ref, frame_ref, *refs):
    windows, kept_refs, refs = refs[:9], refs[9:12], refs[12:]
    attended_refs, (inverse_ref, window_ref, scores_ref, weights_ref, sems, in_sems) = refs[:2], refs[2:]
    pairs, start = [], 0
    for window in windows:
        pairs.append((window, window_ref.at[pl.ds(start, window.shape[0])]))
        start += window.shape[0]
    arriving = dict(zip(range(0, SLOTS, 2), copy_all(pairs, in_sems)))
    copies = []

    def bias_of(f, s):
        return jnp.where(allowed_ref[f, s] > 0, 0.0, MASKED)

    factor = SCORE_SCALE * LOG2_E
    queries = [q_mine_ref[...], frame_ref[2 * TILE : 3 * TILE, :]]
    highest = [jnp.full((8, TILE), -jnp.inf, jnp.float32) for _ in range(2)]
    for first in range(0, SLOTS, 6):
        for s in range(first, first + 6):
            if s in arriving:
                arriving[s].wait()
        keys = window_ref[first : first + 6, 0].reshape(6 * TILE, HD)
        for f in range(2):
            scores_ref[f, first : first + 6] = contract_last(keys, queries[f]).reshape(6, TILE, TILE)
            for s in range(first, first + 6):
                top = jnp.max(scores_ref[f, s].reshape(TILE // 8, 8, TILE), axis=0) * factor
                highest[f] = jnp.maximum(highest[f], top + bias_of(f, s))
    for f in range(2):
        cols = slice(f * TILE, (f + 1) * TILE)
        limit = jnp.max(highest[f], axis=0, keepdims=True)
        total = jnp.zeros((8, TILE), jnp.float32)
        summed = jnp.zeros((HD, TILE), jnp.float32)
        for first in range(0, SLOTS, 6):
            for s in range(first, first + 6):
                weights = jnp.exp2(scores_ref[f, s] * factor + (bias_of(f, s) - limit))
                weights_ref[f, s] = weights.astype(jnp.bfloat16)
            value = window_ref[first : first + 6, 1].reshape(6 * TILE, HD)
            block = weights_ref[f, first : first + 6].reshape(6 * TILE, TILE)
            summed = summed + contract_first(value, block)
            total = total + contract_first(jnp.full((6 * TILE, 8), 0.125, jnp.bfloat16), block)
        inverse = 1.0 / jnp.sum(total, axis=0, keepdims=True)
        inverse_ref[:, cols] = jnp.broadcast_to(inverse, (8, TILE))
        attended_refs[f][...] = (summed * inverse).T.astype(jnp.bfloat16)
        start = 0
        for part, kept_ref in enumerate(kept_refs):
            count = kept_ref.shape[1]
            copy = pltpu.make_async_copy(
                weights_ref.at[f, pl.ds(start, count)], kept_ref.at[f], sems.at[f, part]
            )
            copy.start()
            copies.append(copy)
            start += count
    for copy in copies:
        copy.wait()


def backward_kernel(
    count, last, q_mine_ref, frame_ref, grad_mine_ref, grad_got_ref, own_ref, other_ref, inverse_ref, *refs
):
    before_ref, kept_ref, *refs = refs
    windows, (grad_q_ref, *parts) = refs[:count], refs[count : 2 * count + 1]
    weights_ref, sems, *window_refs = refs[2 * count + 1 :]
    copies = copy_all([(kept_ref, weights_ref), *zip(windows, window_refs)], sems)
    queries = [q_mine_ref[...], frame_ref[2 * TILE : 3 * TILE, :]]
    grads = [grad_mine_ref[...], grad_got_ref[...]]
    deltas = []
    for f in range(2):
        product = grads[f].astype(jnp.float32) * (own_ref, other_ref)[f][...].astype(jnp.float32)
        deltas.append(jnp.sum(product.T, axis=0, keepdims=True))
    for copy in copies:
        copy.wait()
    slots = slot_refs(window_refs)
    outs = slot_refs(parts)
    span = len(slots) * TILE
    keys = jnp.concatenate([ref[index, 0] for ref, index in slots])
    values = jnp.concatenate([ref[index, 1] for ref, index in slots])
    grad_q, grad_keys, grad_values = [], 0.0, 0.0
    for f in range(2):
        cols = slice(f * TILE, (f + 1) * TILE)
        dprob = contract_last(values, grads[f])
        probs = weights_ref[f].reshape(span, TILE).astype(jnp.float32) * inverse_ref[0:1, cols]
        dscore = (probs * (dprob - deltas[f])).astype(jnp.bfloat16)
        grad_keys = grad_keys + contract_inner(dscore, queries[f])
        grad_values = grad_values + contract_inner(probs.astype(jnp.bfloat16), grads[f])
        grad_q.append(before_ref[f] + contract_first(keys, dscore))
    for s, (out, index) in enumerate(outs):
        rows = slice(s * TILE, (s + 1) * TILE)
        out[index, 0] = (grad_keys[rows] * SCORE_SCALE).astype(jnp.bfloat16)
        out[index, 1] = grad_values[rows].astype(jnp.bfloat16)
    for f in range(2):
        if last:
            grad_q_ref[f] = (grad_q[f] * SCORE_SCALE).T.astype(jnp.bfloat16)
        else:
            grad_q_ref[f] = grad_q[f]


def project_kernel(*refs):
    attended_refs, pack_refs, out_ref = refs[:4], refs[4:8], refs[8]
    for block in range(8):
        cols = slice(block * TILE, (block + 1) * TILE)
        total = jnp.zeros((TILE, TILE), jnp.float32)
        for attended_ref, pack_ref in zip(attended_refs, pack_refs):
            total = total + contract_inner(attended_ref[...], pack_ref[:, cols])
        out_ref[:, cols] = total.astype(jnp.bfloat16)


def residue_kernel(place_ref, mine_ref, other_ref, weight_ref, *refs):
    teacher_refs, (student_ref, mine_grad_ref, other_grad_ref) = refs[:4], refs[4:]
    row, core = place_ref[1], place_ref[2]
    grad = jnp.zeros((TILE, TILE), jnp.float32)
    for side in range(2):
        for back in range(4):
            group = lax.rem(row + 4 - back, 4) * 2 + (core if side == 0 else 1 - core)
            cols = pl.ds(pl.multiple_of(group * TILE, TILE), TILE)
            student = mine_ref[:, cols].astype(jnp.float32) + other_ref[:, cols].astype(jnp.float32)
            student = student.astype(jnp.bfloat16)
            if side == 0 and back == 0:
                student_ref[...] = student
            teacher = teacher_refs[back][:, side * TILE : (side + 1) * TILE]
            residue = (student.astype(jnp.float32) - teacher.astype(jnp.float32)).astype(jnp.bfloat16)
            grad = grad + contract_last(residue, weight_ref[:, cols])
    mine_grad_ref[...] = grad[:, :HD].astype(jnp.bfloat16)
    other_grad_ref[...] = grad[:, HD:].astype(jnp.bfloat16)


def merge_kernel(part_ref, right_ref, left_ref, third_ref, out_ref):
    out_ref[...] = sum_of(part_ref[...], right_ref[...], left_ref[...], third_ref[...]).astype(jnp.bfloat16)


def far_kernel(part_ref, right_ref, left_ref, out_ref):
    out_ref[...] = sum_of(part_ref[...], right_ref[...], left_ref[...]).astype(jnp.bfloat16)


def frame_kernel(part_ref, right_ref, left_ref, row_ref, grad_q_ref, frame_ref):
    total = sum_of(part_ref[1], right_ref[1], left_ref[1], row_ref[1]).astype(jnp.bfloat16)
    frame_ref[0] = total[0]
    frame_ref[1] = total[1]
    frame_ref[2] = grad_q_ref[1]


def join_kernel(place_ref, part_ref, right_ref, left_ref, row_ref, grad_q_ref, frame_ref, *outs):
    first = pl.multiple_of(place_ref[0] * HD, HD)
    mine, other = pl.ds(first, HD), pl.ds(pl.multiple_of(HD - first, HD), HD)
    own = sum_of(part_ref[0], right_ref[0], left_ref[0], row_ref[0]).astype(jnp.bfloat16)
    outs[0][:, mine] = grad_q_ref[0]
    outs[0][:, other] = frame_ref[2]
    for index in range(2):
        outs[1 + index][:, mine] = own[index]
        outs[1 + index][:, other] = frame_ref[index]


def vmem_specs(count):
    return [pl.BlockSpec(memory_space=pltpu.VMEM) for _ in range(count)]


def any_specs(count):
    return [pl.BlockSpec(memory_space=pl.ANY) for _ in range(count)]


def place_spec():
    return [pl.BlockSpec(memory_space=pltpu.SMEM)]


def shape(*dims, dtype=jnp.bfloat16):
    return jax.ShapeDtypeStruct(dims, dtype)


def simple(kernel, name, out_shape, *args, place=None, limit=8):
    head = [] if place is None else [place]
    return pl.pallas_call(
        kernel,
        out_shape=tuple(out_shape),
        in_specs=place_spec() * len(head) + vmem_specs(len(args)),
        out_specs=tuple(vmem_specs(len(out_shape))),
        compiler_params=pltpu.CompilerParams(vmem_limit_bytes=limit * 1024 * 1024),
        cost_estimate=pl.CostEstimate(flops=1_000_000, bytes_accessed=2_000_000, transcendentals=0),
        name=name,
    )(*head, *args)


def forward(allowed, q_mine, frame, windows):
    kept = [shape(2, 6, TILE, TILE) for _ in range(3)]
    return pl.pallas_call(
        forward_kernel,
        out_shape=(*kept, shape(TILE, HD), shape(TILE, HD), shape(8, 2 * TILE, dtype=jnp.float32)),
        in_specs=place_spec() + vmem_specs(2) + any_specs(len(windows)),
        out_specs=tuple(any_specs(3) + vmem_specs(3)),
        scratch_shapes=[
            pltpu.VMEM((SLOTS, 2, TILE, HD), jnp.bfloat16),
            pltpu.VMEM((2, SLOTS, TILE, TILE), jnp.float32),
            pltpu.VMEM((2, SLOTS, TILE, TILE), jnp.bfloat16),
            pltpu.SemaphoreType.DMA((2, 3)),
            pltpu.SemaphoreType.DMA((9,)),
        ],
        compiler_params=pltpu.CompilerParams(vmem_limit_bytes=18 * 1024 * 1024),
        cost_estimate=pl.CostEstimate(flops=3_000_000_000, bytes_accessed=8_000_000, transcendentals=2_400_000),
        name="attend",
    )(allowed, q_mine, frame, *windows)


def backward(common, before, weights, windows, last=False):
    if last:
        out_shape = [shape(2, TILE, HD)]
    else:
        out_shape = [shape(2, HD, TILE, dtype=jnp.float32)]
    out_shape += [shape(*window.shape) for window in windows]
    blocks = 2 * weights.shape[1]
    return pl.pallas_call(
        functools.partial(backward_kernel, len(windows), last),
        out_shape=tuple(out_shape),
        in_specs=vmem_specs(len(common) + 1) + any_specs(1 + len(windows)),
        out_specs=tuple(vmem_specs(len(out_shape))),
        scratch_shapes=[
            pltpu.VMEM(weights.shape, jnp.bfloat16),
            pltpu.SemaphoreType.DMA((1 + len(windows),)),
            *[pltpu.VMEM(window.shape, jnp.bfloat16) for window in windows],
        ],
        compiler_params=pltpu.CompilerParams(vmem_limit_bytes=10 * 1024 * 1024),
        cost_estimate=pl.CostEstimate(
            flops=blocks * 8 * TILE * TILE * HD, bytes_accessed=blocks * 300_000, transcendentals=0
        ),
        name="attend_back",
    )(*common, before, weights, *windows)


def project(attended, packs):
    return pl.pallas_call(
        project_kernel,
        in_specs=vmem_specs(8),
        out_specs=pl.BlockSpec(memory_space=pltpu.VMEM),
        out_shape=jax.ShapeDtypeStruct((TILE, 8 * TILE), jnp.bfloat16),
        compiler_params=pltpu.CompilerParams(vmem_limit_bytes=10 * 1024 * 1024),
        cost_estimate=pl.CostEstimate(flops=1_100_000_000, bytes_accessed=6_000_000, transcendentals=0),
        name="project",
    )(*attended, *packs)


def residue_grad(place, mine, other, packs):
    out_shape = [shape(TILE, TILE), shape(TILE, HD), shape(TILE, HD)]
    return pl.pallas_call(
        residue_kernel,
        grid=(1,),
        out_shape=tuple(out_shape),
        in_specs=place_spec()
        + vmem_specs(2)
        + [pl.BlockSpec((TILE, 8 * TILE), lambda i: (0, 0))]
        + [pl.BlockSpec((TILE, 2 * TILE), lambda i: (0, 4)) for _ in packs],
        out_specs=tuple(vmem_specs(len(out_shape))),
        compiler_params=pltpu.CompilerParams(vmem_limit_bytes=10 * 1024 * 1024),
        cost_estimate=pl.CostEstimate(flops=300_000_000, bytes_accessed=5_000_000, transcendentals=0),
        name="residue",
    )(place, mine, other, packs[0], *packs)


def column_shift(value, step, lines):
    pairs = [
        (line * TW + col, line * TW + col + step)
        for line in lines
        for col in range(TW)
        if 0 <= col + step < TW
    ]
    return lax.ppermute(value, ("xr", "zr", "zc"), pairs)


ALL_LINES = (0, 1, 2, 3)
MIDDLE_LINES = (1, 2)
SWAP = [(0, 1), (1, 0)]


def slot_tiles(frame, xr, zr, zc):
    tiles = []
    for row, live in ((2 * xr + zr, True), (2 * xr + 1 - zr, True), (2 - xr, xr != zr)):
        for step in (0, -1, 1):
            col = zc + step
            inside = (col >= 0) & (col < TW) & live
            for f in (frame, 1 - frame):
                tiles.append(jnp.where(inside, f * 32 + row * TW + col, -2))
    return jnp.stack(tiles)


def beside(value, lines):
    return column_shift(value, 1, lines), column_shift(value, -1, lines)


def from_rows(value):
    return [lax.ppermute(value, "y", [(i, (i + step) % 4) for i in range(4)]) for step in (1, 2, 3)]


def sum_of(*terms):
    total = terms[0].astype(jnp.float32)
    for term in terms[1:]:
        total = total + term.astype(jnp.float32)
    return total


def body(queries, keys, values, out_weight, teacher, block_lists):
    xf, xr, zr, zc = (lax.axis_index(axis) for axis in TILE_AXES)
    place = jnp.stack([xf, lax.axis_index("y"), lax.axis_index("core")]).astype(jnp.int32)

    kv_mine, kv_other, q_mine, q_other = prepare(place, queries, keys, values)

    def listed(head, frame):
        lists = lax.dynamic_index_in_dim(block_lists[:, 0], head, 0, keepdims=False)
        return jnp.any(lists[:, None] == slot_tiles(frame, xr, zr, zc)[None, :], axis=0)

    mask_row = jnp.pad(listed(1 - xf, 1 - xf).astype(jnp.bfloat16), (0, HD - SLOTS))
    message = jnp.concatenate(
        [kv_other.reshape(2 * TILE, HD), q_other, jnp.broadcast_to(mask_row[None], (16, HD))]
    )
    xf_got = lax.ppermute(message, "xf", SWAP)
    allowed = jnp.stack([listed(xf, xf), xf_got[3 * TILE, :SLOTS] > 0.5]).astype(jnp.int32)

    pair = simple(pair_kernel, "pair", [shape(2, 2, TILE, HD)], kv_mine, xf_got)[0]
    row = lax.ppermute(pair, "zr", SWAP)
    third = lax.ppermute(row, ("xr", "zr"), [(0, 2), (3, 1)])
    own_windows = (pair, *beside(pair, ALL_LINES))
    row_windows = (row, *beside(row, ALL_LINES))
    third_windows = (third, *beside(third, MIDDLE_LINES))

    weight_heads = out_weight.reshape(2, HD, 8 * TILE)
    first_head = jnp.where(xf == 0, weight_heads[0], weight_heads[1])
    second_head = jnp.where(xf == 0, weight_heads[1], weight_heads[0])
    far_teacher = lax.ppermute(teacher, "core", SWAP)
    first_head, _ = lax.optimization_barrier((first_head, xf_got))
    pack = jnp.concatenate([jnp.concatenate([first_head, second_head]), teacher, far_teacher], axis=1)
    ring = [(i, (i + 1) % 4) for i in range(4)]
    up = lax.ppermute(pack, "y", ring)
    down = lax.ppermute(pack, "y", [(i, (i + 3) % 4) for i in range(4)])
    across = lax.ppermute(up, "y", ring)
    packs = [pack, up, across, down]

    *weights, own, other, inverse = forward(
        allowed, q_mine, xf_got, own_windows + row_windows + third_windows
    )

    got = lax.ppermute(other, "xf", SWAP)
    attended = jnp.concatenate([own, got], axis=1)
    partial_mine = project([attended] + from_rows(attended), packs)
    partial_other = lax.ppermute(partial_mine, "core", SWAP)
    student, grad_mine, grad_other = residue_grad(place, partial_mine, partial_other, packs)
    grad_got = lax.ppermute(grad_other, "xf", SWAP)

    own_weights, row_weights, third_weights = weights
    common = (q_mine, xf_got, grad_mine, grad_got, own, other, inverse)
    before = jnp.zeros((2, HD, TILE), jnp.float32)
    before, far, far_left, far_right = backward(common, before, third_weights, third_windows)
    before, part, part_left, part_right = backward(common, before, row_weights, row_windows)
    grad_query, near, near_left, near_right = backward(common, before, own_weights, own_windows, last=True)

    def returned(left, right, lines):
        return column_shift(left, -1, lines), column_shift(right, 1, lines)

    far_sum = simple(
        far_kernel, "far_sum", [shape(2, 2, TILE, HD)], far, *returned(far_left, far_right, MIDDLE_LINES)
    )[0]
    third_back = lax.ppermute(far_sum, ("xr", "zr"), [(2, 0), (1, 3)])
    row_sum = simple(
        merge_kernel,
        "merge",
        [shape(2, 2, TILE, HD)],
        part,
        *returned(part_left, part_right, ALL_LINES),
        third_back,
    )[0]
    row_back = lax.ppermute(row_sum, "zr", SWAP)
    from_right, from_left = returned(near_left, near_right, ALL_LINES)
    sums = (near, from_right, from_left, row_back, grad_query)
    frame_sum = simple(frame_kernel, "frame_sum", [shape(3, TILE, HD)], *sums)[0]
    xf_back = lax.ppermute(frame_sum, "xf", SWAP)
    grad_queries, grad_keys, grad_values = simple(
        join_kernel, "join", [shape(TILE, TILE)] * 3, *sums, xf_back, place=place
    )
    return student, grad_queries, grad_keys, grad_values


def solution(mesh):
    split = Mesh(mesh.devices.reshape(2, 2, 2, 8, 4, 2), TILE_AXES + HEAD_AXES)
    both = P(TILE_AXES, HEAD_AXES)
    return jax.shard_map(
        body,
        mesh=split,
        in_specs=(both, both, both, P(HEAD_AXES, None), both, P(HEAD_AXES, TILE_AXES, None)),
        out_specs=(both, both, both, both),
        check_vma=False,
    )
```

```python
import functools

import jax
import jax.numpy as jnp
from jax import lax
from jax.experimental import pallas as pl
from jax.experimental.pallas import tpu as pltpu
from jax.sharding import Mesh, PartitionSpec as P

HD = 128
TW = 8
TILE = 256
SLOTS = 18
MASKED = -1e30
SCORE_SCALE = HD ** (-0.5)
LOG2_E = 1.4426950408889634

TILE_AXES = ("xf", "xr", "zr", "zc")
HEAD_AXES = ("y", "core")


def contract_last(left, right):
    return lax.dot_general(left, right, (((1,), (1,)), ((), ())), preferred_element_type=jnp.float32)


def contract_first(left, right):
    return lax.dot_general(left, right, (((0,), (0,)), ((), ())), preferred_element_type=jnp.float32)


def contract_inner(left, right):
    return lax.dot_general(left, right, (((1,), (0,)), ((), ())), preferred_element_type=jnp.float32)


def slot_refs(refs):
    return [(ref, index) for ref in refs for index in range(ref.shape[0])]


def copy_all(pairs, sems):
    copies = [pltpu.make_async_copy(source, target, sems.at[i]) for i, (source, target) in enumerate(pairs)]
    for copy in copies:
        copy.start()
    return copies


def prepare_kernel(
    place_ref, queries_ref, keys_ref, values_ref, mine_ref, other_ref, q_mine_ref, q_other_ref, in_ref, sems
):
    sources = (keys_ref, values_ref, queries_ref)
    copies = copy_all([(source, in_ref.at[i]) for i, source in enumerate(sources)], sems)
    first = pl.multiple_of(place_ref[0] * HD, HD)
    mine, other = pl.ds(first, HD), pl.ds(pl.multiple_of(HD - first, HD), HD)
    for index in range(2):
        copies[index].wait()
        mine_ref[index] = in_ref[index, :, mine]
        other_ref[index] = in_ref[index, :, other]
    copies[2].wait()
    q_mine_ref[...] = in_ref[2, :, mine]
    q_other_ref[...] = in_ref[2, :, other]


def prepare(place, queries, keys, values):
    out_shape = [shape(2, TILE, HD)] * 2 + [shape(TILE, HD)] * 2
    return pl.pallas_call(
        prepare_kernel,
        out_shape=tuple(out_shape),
        in_specs=place_spec() + [pl.BlockSpec(memory_space=pltpu.HBM)] * 3,
        out_specs=tuple(vmem_specs(len(out_shape))),
        scratch_shapes=[pltpu.VMEM((3, TILE, TILE), jnp.bfloat16), pltpu.SemaphoreType.DMA((3,))],
        compiler_params=pltpu.CompilerParams(vmem_limit_bytes=8 * 1024 * 1024),
        cost_estimate=pl.CostEstimate(flops=1_000_000, bytes_accessed=2_000_000, transcendentals=0),
        name="prepare",
    )(place, queries, keys, values)


def pair_kernel(mine_ref, frame_ref, pair_ref):
    pair_ref[0] = mine_ref[...]
    for part in range(2):
        pair_ref[1, part] = frame_ref[part * TILE : (part + 1) * TILE, :]


def forward_kernel(count, last, allowed_ref, q_mine_ref, frame_ref, *refs):
    groups = range(3 - count, 3) if last else range(count)
    windows, refs = refs[: 3 * count], refs[3 * count :]
    if last:
        (top_before_ref, total_before_ref, summed_before_ref), refs = refs[:3], refs[3:]
    kept_refs, refs = refs[:count], refs[count:]
    if last:
        (*attended_refs, spread_ref, inverse_before_ref, inverse_ref), refs = refs[:5], refs[5:]
    else:
        (top_ref, total_ref, summed_ref), refs = refs[:3], refs[3:]
    window_ref, scores_ref, weights_ref, sems, in_sems = refs
    pairs = [(window, window_ref.at[pl.ds(2 * i, 2)]) for i, window in enumerate(windows)]
    arriving = copy_all(pairs, in_sems)
    copies = []

    def bias_of(f, s):
        return jnp.where(allowed_ref[f, 6 * groups[0] + s] > 0, 0.0, MASKED)

    factor = SCORE_SCALE * LOG2_E
    queries = [q_mine_ref[...], frame_ref[2 * TILE : 3 * TILE, :]]
    highest = [jnp.full((8, TILE), 0.1 * MASKED, jnp.float32) for _ in range(2)]
    for group in range(count):
        for copy in arriving[3 * group : 3 * group + 3]:
            copy.wait()
        first = 6 * group
        keys = window_ref[first : first + 6, 0].reshape(6 * TILE, HD)
        for f in range(2):
            scores_ref[f, first : first + 6] = contract_last(keys, queries[f]).reshape(6, TILE, TILE)
            for s in range(first, first + 6):
                top = jnp.max(scores_ref[f, s].reshape(TILE // 8, 8, TILE), axis=0) * factor
                highest[f] = jnp.maximum(highest[f], top + bias_of(f, s))
    for f in range(2):
        cols = slice(f * TILE, (f + 1) * TILE)
        limit = jnp.max(highest[f], axis=0, keepdims=True)
        total = jnp.zeros((8, TILE), jnp.float32)
        summed = jnp.zeros((HD, TILE), jnp.float32)
        for group in range(count):
            first = 6 * group
            for s in range(first, first + 6):
                weights = jnp.exp2(scores_ref[f, s] * factor + (bias_of(f, s) - limit))
                weights_ref[f, s] = weights.astype(jnp.bfloat16)
            value = window_ref[first : first + 6, 1].reshape(6 * TILE, HD)
            block = weights_ref[f, first : first + 6].reshape(6 * TILE, TILE)
            summed = summed + contract_first(value, block)
            total = total + contract_first(jnp.full((6 * TILE, 8), 0.125, jnp.bfloat16), block)
            copy = pltpu.make_async_copy(weights_ref.at[f, pl.ds(first, 6)], kept_refs[group].at[f], sems.at[f, group])
            copy.start()
            copies.append(copy)
        total = jnp.sum(total, axis=0, keepdims=True)
        if not last:
            top_ref[:, cols] = jnp.broadcast_to(limit, (8, TILE))
            total_ref[:, cols] = jnp.broadcast_to(total, (8, TILE))
            summed_ref[f] = summed
            continue
        limit_before = top_before_ref[0:1, cols]
        joint = jnp.maximum(limit, limit_before)
        share, share_before = jnp.exp2(limit - joint), jnp.exp2(limit_before - joint)
        inverse = 1.0 / (total * share + total_before_ref[0:1, cols] * share_before)
        inverse_ref[:, cols] = jnp.broadcast_to(inverse * share, (8, TILE))
        inverse_before_ref[:, cols] = jnp.broadcast_to(inverse * share_before, (8, TILE))
        attended = (summed * (inverse * share) + summed_before_ref[f] * (inverse * share_before)).T
        attended = attended.astype(jnp.bfloat16)
        attended_refs[f][...] = attended
        frame = allowed_ref[0, SLOTS]
        for peer in range(4):
            spread_ref[frame if f == 0 else 1 - frame, peer] = attended
    for copy in copies:
        copy.wait()


def backward_kernel(
    count, last, q_mine_ref, frame_ref, grad_mine_ref, grad_got_ref, own_ref, other_ref, inverse_ref, *refs
):
    before_ref, kept_ref, *refs = refs
    windows, (grad_q_ref, *parts) = refs[:count], refs[count : 2 * count + 1]
    weights_ref, sems, *window_refs = refs[2 * count + 1 :]
    copies = copy_all([(kept_ref, weights_ref), *zip(windows, window_refs)], sems)
    queries = [q_mine_ref[...], frame_ref[2 * TILE : 3 * TILE, :]]
    grads = [grad_mine_ref[...], grad_got_ref[...]]
    deltas = []
    for f in range(2):
        product = grads[f].astype(jnp.float32) * (own_ref, other_ref)[f][...].astype(jnp.float32)
        deltas.append(jnp.sum(product.T, axis=0, keepdims=True))
    for copy in copies:
        copy.wait()
    slots = slot_refs(window_refs)
    outs = slot_refs(parts)
    span = len(slots) * TILE
    keys = jnp.concatenate([ref[index, 0] for ref, index in slots])
    values = jnp.concatenate([ref[index, 1] for ref, index in slots])
    grad_q, grad_keys, grad_values = [], 0.0, 0.0
    for f in range(2):
        cols = slice(f * TILE, (f + 1) * TILE)
        dprob = contract_last(values, grads[f])
        probs = weights_ref[f].reshape(span, TILE).astype(jnp.float32) * inverse_ref[0:1, cols]
        dscore = (probs * (dprob - deltas[f])).astype(jnp.bfloat16)
        grad_keys = grad_keys + contract_inner(dscore, queries[f])
        grad_values = grad_values + contract_inner(probs.astype(jnp.bfloat16), grads[f])
        grad_q.append(before_ref[f] + contract_first(keys, dscore))
    for s, (out, index) in enumerate(outs):
        rows = slice(s * TILE, (s + 1) * TILE)
        out[index, 0] = (grad_keys[rows] * SCORE_SCALE).astype(jnp.bfloat16)
        out[index, 1] = grad_values[rows].astype(jnp.bfloat16)
    for f in range(2):
        if last:
            grad_q_ref[f] = (grad_q[f] * SCORE_SCALE).T.astype(jnp.bfloat16)
        else:
            grad_q_ref[f] = grad_q[f]


def project_kernel(place_ref, attended_ref, *refs):
    pack_refs, (out_ref,) = refs[:4], refs[4:]
    frame, row = place_ref[0], place_ref[1]
    pieces = []
    for back in range(4):
        source = lax.rem(row + 4 - back, 4)
        pieces.append(jnp.concatenate([attended_ref[frame, source], attended_ref[1 - frame, source]], axis=1))
    for block in range(8):
        cols = slice(block * TILE, (block + 1) * TILE)
        total = jnp.zeros((TILE, TILE), jnp.float32)
        for rows, pack_ref in zip(pieces, pack_refs):
            total = total + contract_inner(rows, pack_ref[:, cols])
        out_ref[:, cols] = total.astype(jnp.bfloat16)


def residue_kernel(place_ref, mine_ref, other_ref, weight_ref, *refs):
    teacher_refs, (student_ref, mine_grad_ref, other_grad_ref) = refs[:4], refs[4:]
    row, core = place_ref[1], place_ref[2]
    grad = jnp.zeros((TILE, TILE), jnp.float32)
    for side in range(2):
        for back in range(4):
            group = lax.rem(row + 4 - back, 4) * 2 + (core if side == 0 else 1 - core)
            cols = pl.ds(pl.multiple_of(group * TILE, TILE), TILE)
            student = mine_ref[:, cols].astype(jnp.float32) + other_ref[:, cols].astype(jnp.float32)
            student = student.astype(jnp.bfloat16)
            if side == 0 and back == 0:
                student_ref[...] = student
            teacher = teacher_refs[back][:, side * TILE : (side + 1) * TILE]
            residue = (student.astype(jnp.float32) - teacher.astype(jnp.float32)).astype(jnp.bfloat16)
            grad = grad + contract_last(residue, weight_ref[:, cols])
    mine_grad_ref[...] = grad[:, :HD].astype(jnp.bfloat16)
    other_grad_ref[...] = grad[:, HD:].astype(jnp.bfloat16)


def merge_kernel(part_ref, right_ref, left_ref, third_ref, out_ref):
    out_ref[...] = sum_of(part_ref[...], right_ref[...], left_ref[...], third_ref[...]).astype(jnp.bfloat16)


def widen_kernel(part_ref, out_ref):
    out_ref[...] = part_ref[...].astype(jnp.float32)


def far_kernel(part_ref, right_ref, left_ref, out_ref):
    out_ref[...] = sum_of(part_ref[...], right_ref[...], left_ref[...]).astype(jnp.bfloat16)


def frame_kernel(part_ref, right_ref, left_ref, row_ref, grad_q_ref, frame_ref):
    total = sum_of(part_ref[1], right_ref[1], left_ref[1], row_ref[1]).astype(jnp.bfloat16)
    frame_ref[0] = total[0]
    frame_ref[1] = total[1]
    frame_ref[2] = grad_q_ref[1]


def join_kernel(place_ref, part_ref, right_ref, left_ref, row_ref, grad_q_ref, frame_ref, *outs):
    first = pl.multiple_of(place_ref[0] * HD, HD)
    mine, other = pl.ds(first, HD), pl.ds(pl.multiple_of(HD - first, HD), HD)
    own = sum_of(part_ref[0], right_ref[0], left_ref[0], row_ref[0]).astype(jnp.bfloat16)
    outs[0][:, mine] = grad_q_ref[0]
    outs[0][:, other] = frame_ref[2]
    for index in range(2):
        outs[1 + index][:, mine] = own[index]
        outs[1 + index][:, other] = frame_ref[index]


def vmem_specs(count):
    return [pl.BlockSpec(memory_space=pltpu.VMEM) for _ in range(count)]


def any_specs(count):
    return [pl.BlockSpec(memory_space=pl.ANY) for _ in range(count)]


def place_spec():
    return [pl.BlockSpec(memory_space=pltpu.SMEM)]


def shape(*dims, dtype=jnp.bfloat16):
    return jax.ShapeDtypeStruct(dims, dtype)


def simple(kernel, name, out_shape, *args, place=None, limit=8, flops=1_000_000):
    head = [] if place is None else [place]
    return pl.pallas_call(
        kernel,
        out_shape=tuple(out_shape),
        in_specs=place_spec() * len(head) + vmem_specs(len(args)),
        out_specs=tuple(vmem_specs(len(out_shape))),
        compiler_params=pltpu.CompilerParams(vmem_limit_bytes=limit * 1024 * 1024),
        cost_estimate=pl.CostEstimate(flops=flops, bytes_accessed=2_000_000, transcendentals=0),
        name=name,
    )(*head, *args)


def forward(allowed, q_mine, frame, windows, before=()):
    count, last = len(windows) // 3, bool(before)
    rows = shape(8, 2 * TILE, dtype=jnp.float32)
    if last:
        out_shape = [shape(TILE, HD), shape(TILE, HD), shape(2, 4, TILE, HD), rows, rows]
    else:
        out_shape = [rows, rows, shape(2, HD, TILE, dtype=jnp.float32)]
    return pl.pallas_call(
        functools.partial(forward_kernel, count, last),
        out_shape=tuple([shape(2, 6, TILE, TILE)] * count + out_shape),
        in_specs=place_spec() + vmem_specs(2) + any_specs(len(windows)) + vmem_specs(len(before)),
        out_specs=tuple(any_specs(count) + vmem_specs(len(out_shape))),
        scratch_shapes=[
            pltpu.VMEM((6 * count, 2, TILE, HD), jnp.bfloat16),
            pltpu.VMEM((2, 6 * count, TILE, TILE), jnp.float32),
            pltpu.VMEM((2, 6 * count, TILE, TILE), jnp.bfloat16),
            pltpu.SemaphoreType.DMA((2, count)),
            pltpu.SemaphoreType.DMA((3 * count,)),
        ],
        compiler_params=pltpu.CompilerParams(vmem_limit_bytes=18 * 1024 * 1024),
        cost_estimate=pl.CostEstimate(
            flops=count * 1_000_000_000, bytes_accessed=count * 2_700_000, transcendentals=count * 800_000
        ),
        name="attend",
    )(allowed, q_mine, frame, *windows, *before)


def backward(common, before, weights, windows, last=False):
    if last:
        out_shape = [shape(2, TILE, HD)]
    else:
        out_shape = [shape(2, HD, TILE, dtype=jnp.float32)]
    out_shape += [shape(*window.shape) for window in windows]
    blocks = 2 * weights.shape[1]
    return pl.pallas_call(
        functools.partial(backward_kernel, len(windows), last),
        out_shape=tuple(out_shape),
        in_specs=vmem_specs(len(common) + 1) + any_specs(1 + len(windows)),
        out_specs=tuple(vmem_specs(len(out_shape))),
        scratch_shapes=[
            pltpu.VMEM(weights.shape, jnp.bfloat16),
            pltpu.SemaphoreType.DMA((1 + len(windows),)),
            *[pltpu.VMEM(window.shape, jnp.bfloat16) for window in windows],
        ],
        compiler_params=pltpu.CompilerParams(vmem_limit_bytes=10 * 1024 * 1024),
        cost_estimate=pl.CostEstimate(
            flops=blocks * 8 * TILE * TILE * HD, bytes_accessed=blocks * 300_000, transcendentals=0
        ),
        name="attend_back",
    )(*common, before, weights, *windows)


def project(place, attended, packs):
    return pl.pallas_call(
        project_kernel,
        in_specs=place_spec() + vmem_specs(5),
        out_specs=pl.BlockSpec(memory_space=pltpu.VMEM),
        out_shape=jax.ShapeDtypeStruct((TILE, 8 * TILE), jnp.bfloat16),
        compiler_params=pltpu.CompilerParams(vmem_limit_bytes=10 * 1024 * 1024),
        cost_estimate=pl.CostEstimate(flops=1_100_000_000, bytes_accessed=6_000_000, transcendentals=0),
        name="project",
    )(place, attended, *packs)


def residue_grad(place, mine, other, packs):
    out_shape = [shape(TILE, TILE), shape(TILE, HD), shape(TILE, HD)]
    return pl.pallas_call(
        residue_kernel,
        grid=(1,),
        out_shape=tuple(out_shape),
        in_specs=place_spec()
        + vmem_specs(2)
        + [pl.BlockSpec((TILE, 8 * TILE), lambda i: (0, 0))]
        + [pl.BlockSpec((TILE, 2 * TILE), lambda i: (0, 4)) for _ in packs],
        out_specs=tuple(vmem_specs(len(out_shape))),
        compiler_params=pltpu.CompilerParams(vmem_limit_bytes=10 * 1024 * 1024),
        cost_estimate=pl.CostEstimate(flops=300_000_000, bytes_accessed=5_000_000, transcendentals=0),
        name="residue",
    )(place, mine, other, packs[0], *packs)


def column_shift(value, step, lines):
    pairs = [
        (line * TW + col, line * TW + col + step)
        for line in lines
        for col in range(TW)
        if 0 <= col + step < TW
    ]
    return lax.ppermute(value, ("xr", "zr", "zc"), pairs)


ALL_LINES = (0, 1, 2, 3)
MIDDLE_LINES = (1, 2)
SWAP = [(0, 1), (1, 0)]


def slot_tiles(frame, xr, zr, zc):
    tiles = []
    for row, live in ((2 * xr + zr, True), (2 * xr + 1 - zr, True), (2 - xr, xr != zr)):
        for step in (0, -1, 1):
            col = zc + step
            inside = (col >= 0) & (col < TW) & live
            for f in (frame, 1 - frame):
                tiles.append(jnp.where(inside, f * 32 + row * TW + col, -2))
    return jnp.stack(tiles)


def beside(value, lines):
    return column_shift(value, 1, lines), column_shift(value, -1, lines)


def from_rows(value):
    return [lax.ppermute(value, "y", [(i, (i + step) % 4) for i in range(4)]) for step in (1, 2, 3)]


def sum_of(*terms):
    total = terms[0].astype(jnp.float32)
    for term in terms[1:]:
        total = total + term.astype(jnp.float32)
    return total


def body(queries, keys, values, out_weight, teacher, block_lists):
    xf, xr, zr, zc = (lax.axis_index(axis) for axis in TILE_AXES)
    place = jnp.stack([xf, lax.axis_index("y"), lax.axis_index("core")]).astype(jnp.int32)

    kv_mine, kv_other, q_mine, q_other = prepare(place, queries, keys, values)

    def listed(head, frame):
        lists = lax.dynamic_index_in_dim(block_lists[:, 0], head, 0, keepdims=False)
        return jnp.any(lists[:, None] == slot_tiles(frame, xr, zr, zc)[None, :], axis=0)

    mask_row = jnp.pad(listed(1 - xf, 1 - xf).astype(jnp.bfloat16), (0, HD - SLOTS))
    message = jnp.concatenate(
        [kv_other.reshape(2 * TILE, HD), q_other, jnp.broadcast_to(mask_row[None], (16, HD))]
    )
    xf_got = lax.ppermute(message, "xf", SWAP)
    allowed = jnp.stack([listed(xf, xf), xf_got[3 * TILE, :SLOTS] > 0.5]).astype(jnp.int32)
    allowed = jnp.concatenate([allowed, jnp.broadcast_to(xf.astype(jnp.int32), (2, 1))], axis=1)

    pair = simple(pair_kernel, "pair", [shape(2, 2, TILE, HD)], kv_mine, xf_got)[0]
    row = lax.ppermute(pair, "zr", SWAP)
    third = lax.ppermute(row, ("xr", "zr"), [(0, 2), (3, 1)])
    own_windows = (pair, *beside(pair, ALL_LINES))
    row_windows = (row, *beside(row, ALL_LINES))
    third_windows = (third, *beside(third, MIDDLE_LINES))

    weight_heads = out_weight.reshape(2, HD, 8 * TILE)
    first_head = jnp.where(xf == 0, weight_heads[0], weight_heads[1])
    second_head = jnp.where(xf == 0, weight_heads[1], weight_heads[0])
    far_teacher = lax.ppermute(teacher, "core", SWAP)
    first_head, _ = lax.optimization_barrier((first_head, xf_got))
    pack = jnp.concatenate([jnp.concatenate([first_head, second_head]), teacher, far_teacher], axis=1)
    ring = [(i, (i + 1) % 4) for i in range(4)]
    up = lax.ppermute(pack, "y", ring)
    down = lax.ppermute(pack, "y", [(i, (i + 3) % 4) for i in range(4)])
    across = lax.ppermute(up, "y", ring)
    packs = [pack, up, across, down]

    own_weights, row_weights, *sums_before = forward(allowed, q_mine, xf_got, own_windows + row_windows)
    third_weights, own, other, spread, inverse, inverse_third = forward(
        allowed, q_mine, xf_got, third_windows, sums_before
    )

    gathered = lax.all_to_all(spread.reshape(8, TILE, HD), ("xf", "y"), 0, 0, tiled=True)
    partial_mine = project(place, gathered.reshape(2, 4, TILE, HD), packs)
    partial_other = lax.ppermute(partial_mine, "core", SWAP)
    student, grad_mine, grad_other = residue_grad(place, partial_mine, partial_other, packs)
    grad_got = lax.ppermute(grad_other, "xf", SWAP)

    common = (q_mine, xf_got, grad_mine, grad_got, own, other, inverse)
    common_third = common[:-1] + (inverse_third,)
    before = jnp.zeros((2, HD, TILE), jnp.float32)
    before, far, far_left, far_right = backward(common_third, before, third_weights, third_windows)
    before, part, part_left, part_right = backward(common, before, row_weights, row_windows)
    def returned(left, right, lines):
        return column_shift(left, -1, lines), column_shift(right, 1, lines)

    far_sum = simple(
        far_kernel, "far_sum", [shape(2, 2, TILE, HD)], far, *returned(far_left, far_right, MIDDLE_LINES)
    )[0]
    third_back = lax.ppermute(far_sum, ("xr", "zr"), [(2, 0), (1, 3)])
    row_sum = simple(
        merge_kernel,
        "merge",
        [shape(2, 2, TILE, HD)],
        part,
        *returned(part_left, part_right, ALL_LINES),
        third_back,
    )[0]
    row_back = lax.ppermute(row_sum, "zr", SWAP)
    row_back = simple(widen_kernel, "widen", [shape(2, 2, TILE, HD, dtype=jnp.float32)], row_back, flops=30_000_000_000)[0]
    before, _ = lax.optimization_barrier((before, row_sum))
    grad_query, near, near_left, near_right = backward(common, before, own_weights, own_windows, last=True)
    from_right, from_left = returned(near_left, near_right, ALL_LINES)
    sums = (near, from_right, from_left, row_back, grad_query)
    frame_sum = simple(frame_kernel, "frame_sum", [shape(3, TILE, HD)], *sums)[0]
    xf_back = lax.ppermute(frame_sum, "xf", SWAP)
    grad_queries, grad_keys, grad_values = simple(
        join_kernel, "join", [shape(TILE, TILE)] * 3, *sums, xf_back, place=place
    )
    return student, grad_queries, grad_keys, grad_values


def solution(mesh):
    split = Mesh(mesh.devices.reshape(2, 2, 2, 8, 4, 2), TILE_AXES + HEAD_AXES)
    both = P(TILE_AXES, HEAD_AXES)
    return jax.shard_map(
        body,
        mesh=split,
        in_specs=(both, both, both, P(HEAD_AXES, None), both, P(HEAD_AXES, TILE_AXES, None)),
        out_specs=(both, both, both, both),
        check_vma=False,
    )
```

```python
import functools

import jax
import jax.numpy as jnp
from jax import lax
from jax.experimental import pallas as pl
from jax.experimental.pallas import tpu as pltpu
from jax.sharding import Mesh, PartitionSpec as P

HD = 128
TW = 8
TILE = 256
SLOTS = 18
MASKED = -1e30
SCORE_SCALE = HD ** (-0.5)
LOG2_E = 1.4426950408889634

TILE_AXES = ("xf", "xr", "zr", "zc")
HEAD_AXES = ("y", "core")


def contract_last(left, right):
    return lax.dot_general(left, right, (((1,), (1,)), ((), ())), preferred_element_type=jnp.float32)


def contract_first(left, right):
    return lax.dot_general(left, right, (((0,), (0,)), ((), ())), preferred_element_type=jnp.float32)


def contract_inner(left, right):
    return lax.dot_general(left, right, (((1,), (0,)), ((), ())), preferred_element_type=jnp.float32)


def slot_refs(refs):
    return [(ref, index) for ref in refs for index in range(ref.shape[0])]


def copy_all(pairs, sems):
    copies = [pltpu.make_async_copy(source, target, sems.at[i]) for i, (source, target) in enumerate(pairs)]
    for copy in copies:
        copy.start()
    return copies


def prepare_kernel(
    place_ref, queries_ref, keys_ref, values_ref, mine_ref, other_ref, q_mine_ref, q_other_ref, in_ref, sems
):
    sources = (keys_ref, values_ref, queries_ref)
    copies = copy_all([(source, in_ref.at[i]) for i, source in enumerate(sources)], sems)
    first = pl.multiple_of(place_ref[0] * HD, HD)
    mine, other = pl.ds(first, HD), pl.ds(pl.multiple_of(HD - first, HD), HD)
    for index in range(2):
        copies[index].wait()
        mine_ref[index] = in_ref[index, :, mine]
        other_ref[index] = in_ref[index, :, other]
    copies[2].wait()
    q_mine_ref[...] = in_ref[2, :, mine]
    q_other_ref[...] = in_ref[2, :, other]


def prepare(place, queries, keys, values):
    out_shape = [shape(2, TILE, HD)] * 2 + [shape(TILE, HD)] * 2
    return pl.pallas_call(
        prepare_kernel,
        out_shape=tuple(out_shape),
        in_specs=place_spec() + [pl.BlockSpec(memory_space=pltpu.HBM)] * 3,
        out_specs=tuple(vmem_specs(len(out_shape))),
        scratch_shapes=[pltpu.VMEM((3, TILE, TILE), jnp.bfloat16), pltpu.SemaphoreType.DMA((3,))],
        compiler_params=pltpu.CompilerParams(vmem_limit_bytes=8 * 1024 * 1024),
        cost_estimate=pl.CostEstimate(flops=1_000_000, bytes_accessed=2_000_000, transcendentals=0),
        name="prepare",
    )(place, queries, keys, values)


def pair_kernel(mine_ref, frame_ref, pair_ref):
    pair_ref[0] = mine_ref[...]
    for part in range(2):
        pair_ref[1, part] = frame_ref[part * TILE : (part + 1) * TILE, :]


def forward_kernel(count, last, allowed_ref, q_mine_ref, frame_ref, *refs):
    groups = range(3 - count, 3) if last else range(count)
    windows, refs = refs[: 3 * count], refs[3 * count :]
    if last:
        (top_before_ref, total_before_ref, summed_before_ref), refs = refs[:3], refs[3:]
    kept_refs, refs = refs[:count], refs[count:]
    if last:
        (*attended_refs, spread_ref, inverse_before_ref, inverse_ref), refs = refs[:5], refs[5:]
    else:
        (top_ref, total_ref, summed_ref), refs = refs[:3], refs[3:]
    window_ref, scores_ref, weights_ref, sems, in_sems = refs
    pairs = [(window, window_ref.at[pl.ds(2 * i, 2)]) for i, window in enumerate(windows)]
    arriving = copy_all(pairs, in_sems)
    copies = []

    def bias_of(f, s):
        return jnp.where(allowed_ref[f, 6 * groups[0] + s] > 0, 0.0, MASKED)

    factor = SCORE_SCALE * LOG2_E
    queries = [q_mine_ref[...], frame_ref[2 * TILE : 3 * TILE, :]]
    highest = [jnp.full((8, TILE), 0.1 * MASKED, jnp.float32) for _ in range(2)]
    for group in range(count):
        for copy in arriving[3 * group : 3 * group + 3]:
            copy.wait()
        first = 6 * group
        keys = window_ref[first : first + 6, 0].reshape(6 * TILE, HD)
        for f in range(2):
            scores_ref[f, first : first + 6] = contract_last(keys, queries[f]).reshape(6, TILE, TILE)
            for s in range(first, first + 6):
                top = jnp.max(scores_ref[f, s].reshape(TILE // 8, 8, TILE), axis=0) * factor
                highest[f] = jnp.maximum(highest[f], top + bias_of(f, s))
    for f in range(2):
        cols = slice(f * TILE, (f + 1) * TILE)
        limit = jnp.max(highest[f], axis=0, keepdims=True)
        total = jnp.zeros((8, TILE), jnp.float32)
        summed = jnp.zeros((HD, TILE), jnp.float32)
        for group in range(count):
            first = 6 * group
            for s in range(first, first + 6):
                weights = jnp.exp2(scores_ref[f, s] * factor + (bias_of(f, s) - limit))
                weights_ref[f, s] = weights.astype(jnp.bfloat16)
            value = window_ref[first : first + 6, 1].reshape(6 * TILE, HD)
            block = weights_ref[f, first : first + 6].reshape(6 * TILE, TILE)
            summed = summed + contract_first(value, block)
            total = total + contract_first(jnp.full((6 * TILE, 8), 0.125, jnp.bfloat16), block)
            copy = pltpu.make_async_copy(weights_ref.at[f, pl.ds(first, 6)], kept_refs[group].at[f], sems.at[f, group])
            copy.start()
            copies.append(copy)
        total = jnp.sum(total, axis=0, keepdims=True)
        if not last:
            top_ref[:, cols] = jnp.broadcast_to(limit, (8, TILE))
            total_ref[:, cols] = jnp.broadcast_to(total, (8, TILE))
            summed_ref[f] = summed
            continue
        limit_before = top_before_ref[0:1, cols]
        joint = jnp.maximum(limit, limit_before)
        share, share_before = jnp.exp2(limit - joint), jnp.exp2(limit_before - joint)
        inverse = 1.0 / (total * share + total_before_ref[0:1, cols] * share_before)
        inverse_ref[:, cols] = jnp.broadcast_to(inverse * share, (8, TILE))
        inverse_before_ref[:, cols] = jnp.broadcast_to(inverse * share_before, (8, TILE))
        attended = (summed * (inverse * share) + summed_before_ref[f] * (inverse * share_before)).T
        attended = attended.astype(jnp.bfloat16)
        attended_refs[f][...] = attended
        frame = allowed_ref[0, SLOTS]
        for peer in range(4):
            spread_ref[frame if f == 0 else 1 - frame, peer] = attended
    for copy in copies:
        copy.wait()


def backward_kernel(
    count, last, q_mine_ref, frame_ref, grad_mine_ref, grad_got_ref, own_ref, other_ref, inverse_ref, *refs
):
    before_ref, kept_ref, *refs = refs
    windows, (grad_q_ref, *parts) = refs[:count], refs[count : 2 * count + 1]
    weights_ref, sems, *window_refs = refs[2 * count + 1 :]
    copies = copy_all([(kept_ref, weights_ref), *zip(windows, window_refs)], sems)
    queries = [q_mine_ref[...], frame_ref[2 * TILE : 3 * TILE, :]]
    grads = [grad_mine_ref[...], grad_got_ref[...]]
    deltas = []
    for f in range(2):
        product = grads[f].astype(jnp.float32) * (own_ref, other_ref)[f][...].astype(jnp.float32)
        deltas.append(jnp.sum(product.T, axis=0, keepdims=True))
    for copy in copies:
        copy.wait()
    slots = slot_refs(window_refs)
    outs = slot_refs(parts)
    span = len(slots) * TILE
    keys = jnp.concatenate([ref[index, 0] for ref, index in slots])
    values = jnp.concatenate([ref[index, 1] for ref, index in slots])
    grad_q, grad_keys, grad_values = [], 0.0, 0.0
    for f in range(2):
        cols = slice(f * TILE, (f + 1) * TILE)
        dprob = contract_last(values, grads[f])
        probs = weights_ref[f].reshape(span, TILE).astype(jnp.float32) * inverse_ref[0:1, cols]
        dscore = (probs * (dprob - deltas[f])).astype(jnp.bfloat16)
        grad_keys = grad_keys + contract_inner(dscore, queries[f])
        grad_values = grad_values + contract_inner(probs.astype(jnp.bfloat16), grads[f])
        grad_q.append(before_ref[f] + contract_first(keys, dscore))
    for s, (out, index) in enumerate(outs):
        rows = slice(s * TILE, (s + 1) * TILE)
        out[index, 0] = (grad_keys[rows] * SCORE_SCALE).astype(jnp.bfloat16)
        out[index, 1] = grad_values[rows].astype(jnp.bfloat16)
    for f in range(2):
        if last:
            grad_q_ref[f] = (grad_q[f] * SCORE_SCALE).T.astype(jnp.bfloat16)
        else:
            grad_q_ref[f] = grad_q[f]


def project_kernel(place_ref, attended_ref, *refs):
    pack_refs, (out_ref,) = refs[:4], refs[4:]
    frame, row = place_ref[0], place_ref[1]
    pieces = []
    for back in range(4):
        source = lax.rem(row + 4 - back, 4)
        pieces.append(jnp.concatenate([attended_ref[frame, source], attended_ref[1 - frame, source]], axis=1))
    for block in range(8):
        cols = slice(block * TILE, (block + 1) * TILE)
        total = jnp.zeros((TILE, TILE), jnp.float32)
        for rows, pack_ref in zip(pieces, pack_refs):
            total = total + contract_inner(rows, pack_ref[:, cols])
        out_ref[:, cols] = total.astype(jnp.bfloat16)


def residue_kernel(place_ref, mine_ref, other_ref, weight_ref, *refs):
    teacher_refs, (student_ref, mine_grad_ref, other_grad_ref) = refs[:4], refs[4:]
    row, core = place_ref[1], place_ref[2]
    grad = jnp.zeros((TILE, TILE), jnp.float32)
    for side in range(2):
        for back in range(4):
            group = lax.rem(row + 4 - back, 4) * 2 + (core if side == 0 else 1 - core)
            cols = pl.ds(pl.multiple_of(group * TILE, TILE), TILE)
            student = mine_ref[:, cols].astype(jnp.float32) + other_ref[:, cols].astype(jnp.float32)
            student = student.astype(jnp.bfloat16)
            if side == 0 and back == 0:
                student_ref[...] = student
            teacher = teacher_refs[back][:, side * TILE : (side + 1) * TILE]
            residue = (student.astype(jnp.float32) - teacher.astype(jnp.float32)).astype(jnp.bfloat16)
            grad = grad + contract_last(residue, weight_ref[:, cols])
    mine_grad_ref[...] = grad[:, :HD].astype(jnp.bfloat16)
    other_grad_ref[...] = grad[:, HD:].astype(jnp.bfloat16)


def merge_kernel(part_ref, right_ref, left_ref, third_ref, out_ref):
    out_ref[...] = sum_of(part_ref[...], right_ref[...], left_ref[...], third_ref[...]).astype(jnp.bfloat16)


def widen_kernel(part_ref, out_ref):
    out_ref[...] = part_ref[...].astype(jnp.float32)


def far_kernel(part_ref, right_ref, left_ref, out_ref):
    out_ref[...] = sum_of(part_ref[...], right_ref[...], left_ref[...]).astype(jnp.bfloat16)


def frame_kernel(part_ref, right_ref, left_ref, row_ref, grad_q_ref, frame_ref):
    total = sum_of(part_ref[1], right_ref[1], left_ref[1], row_ref[1]).astype(jnp.bfloat16)
    frame_ref[0] = total[0]
    frame_ref[1] = total[1]
    frame_ref[2] = grad_q_ref[1]


def join_kernel(place_ref, part_ref, right_ref, left_ref, row_ref, grad_q_ref, frame_ref, *outs):
    first = pl.multiple_of(place_ref[0] * HD, HD)
    mine, other = pl.ds(first, HD), pl.ds(pl.multiple_of(HD - first, HD), HD)
    own = sum_of(part_ref[0], right_ref[0], left_ref[0], row_ref[0]).astype(jnp.bfloat16)
    outs[0][:, mine] = grad_q_ref[0]
    outs[0][:, other] = frame_ref[2]
    for index in range(2):
        outs[1 + index][:, mine] = own[index]
        outs[1 + index][:, other] = frame_ref[index]


def vmem_specs(count):
    return [pl.BlockSpec(memory_space=pltpu.VMEM) for _ in range(count)]


def any_specs(count):
    return [pl.BlockSpec(memory_space=pl.ANY) for _ in range(count)]


def place_spec():
    return [pl.BlockSpec(memory_space=pltpu.SMEM)]


def shape(*dims, dtype=jnp.bfloat16):
    return jax.ShapeDtypeStruct(dims, dtype)


def simple(kernel, name, out_shape, *args, place=None, limit=8, flops=1_000_000):
    head = [] if place is None else [place]
    return pl.pallas_call(
        kernel,
        out_shape=tuple(out_shape),
        in_specs=place_spec() * len(head) + vmem_specs(len(args)),
        out_specs=tuple(vmem_specs(len(out_shape))),
        compiler_params=pltpu.CompilerParams(vmem_limit_bytes=limit * 1024 * 1024),
        cost_estimate=pl.CostEstimate(flops=flops, bytes_accessed=2_000_000, transcendentals=0),
        name=name,
    )(*head, *args)


def forward(allowed, q_mine, frame, windows, before=()):
    count, last = len(windows) // 3, bool(before)
    rows = shape(8, 2 * TILE, dtype=jnp.float32)
    if last:
        out_shape = [shape(TILE, HD), shape(TILE, HD), shape(2, 4, TILE, HD), rows, rows]
    else:
        out_shape = [rows, rows, shape(2, HD, TILE, dtype=jnp.float32)]
    return pl.pallas_call(
        functools.partial(forward_kernel, count, last),
        out_shape=tuple([shape(2, 6, TILE, TILE)] * count + out_shape),
        in_specs=place_spec() + vmem_specs(2) + any_specs(len(windows)) + vmem_specs(len(before)),
        out_specs=tuple(any_specs(count) + vmem_specs(len(out_shape))),
        scratch_shapes=[
            pltpu.VMEM((6 * count, 2, TILE, HD), jnp.bfloat16),
            pltpu.VMEM((2, 6 * count, TILE, TILE), jnp.float32),
            pltpu.VMEM((2, 6 * count, TILE, TILE), jnp.bfloat16),
            pltpu.SemaphoreType.DMA((2, count)),
            pltpu.SemaphoreType.DMA((3 * count,)),
        ],
        compiler_params=pltpu.CompilerParams(vmem_limit_bytes=18 * 1024 * 1024),
        cost_estimate=pl.CostEstimate(
            flops=count * 1_000_000_000, bytes_accessed=count * 2_700_000, transcendentals=count * 800_000
        ),
        name="attend",
    )(allowed, q_mine, frame, *windows, *before)


def backward(common, before, weights, windows, last=False):
    if last:
        out_shape = [shape(2, TILE, HD)]
    else:
        out_shape = [shape(2, HD, TILE, dtype=jnp.float32)]
    out_shape += [shape(*window.shape) for window in windows]
    blocks = 2 * weights.shape[1]
    return pl.pallas_call(
        functools.partial(backward_kernel, len(windows), last),
        out_shape=tuple(out_shape),
        in_specs=vmem_specs(len(common) + 1) + any_specs(1 + len(windows)),
        out_specs=tuple(vmem_specs(len(out_shape))),
        scratch_shapes=[
            pltpu.VMEM(weights.shape, jnp.bfloat16),
            pltpu.SemaphoreType.DMA((1 + len(windows),)),
            *[pltpu.VMEM(window.shape, jnp.bfloat16) for window in windows],
        ],
        compiler_params=pltpu.CompilerParams(vmem_limit_bytes=10 * 1024 * 1024),
        cost_estimate=pl.CostEstimate(
            flops=blocks * 8 * TILE * TILE * HD, bytes_accessed=blocks * 300_000, transcendentals=0
        ),
        name="attend_back",
    )(*common, before, weights, *windows)


def project(place, attended, packs):
    return pl.pallas_call(
        project_kernel,
        in_specs=place_spec() + vmem_specs(5),
        out_specs=pl.BlockSpec(memory_space=pltpu.VMEM),
        out_shape=jax.ShapeDtypeStruct((TILE, 8 * TILE), jnp.bfloat16),
        compiler_params=pltpu.CompilerParams(vmem_limit_bytes=10 * 1024 * 1024),
        cost_estimate=pl.CostEstimate(flops=1_100_000_000, bytes_accessed=6_000_000, transcendentals=0),
        name="project",
    )(place, attended, *packs)


def residue_grad(place, mine, other, packs):
    out_shape = [shape(TILE, TILE), shape(TILE, HD), shape(TILE, HD)]
    return pl.pallas_call(
        residue_kernel,
        grid=(1,),
        out_shape=tuple(out_shape),
        in_specs=place_spec()
        + vmem_specs(2)
        + [pl.BlockSpec((TILE, 8 * TILE), lambda i: (0, 0))]
        + [pl.BlockSpec((TILE, 2 * TILE), lambda i: (0, 4)) for _ in packs],
        out_specs=tuple(vmem_specs(len(out_shape))),
        compiler_params=pltpu.CompilerParams(vmem_limit_bytes=10 * 1024 * 1024),
        cost_estimate=pl.CostEstimate(flops=300_000_000, bytes_accessed=5_000_000, transcendentals=0),
        name="residue",
    )(place, mine, other, packs[0], *packs)


def column_swap(value, turn, lines):
    pairs = []
    for line in lines:
        for col in range(turn, TW - 1, 2):
            here = line * TW + col
            pairs += [(here, here + 1), (here + 1, here)]
    return lax.ppermute(value, ("xr", "zr", "zc"), pairs)


ALL_LINES = (0, 1, 2, 3)
MIDDLE_LINES = (1, 2)
SWAP = [(0, 1), (1, 0)]


def slot_tiles(frame, xr, zr, zc):
    toward = 1 - 2 * (zc % 2)
    tiles = []
    for row, live in ((2 * xr + zr, True), (2 * xr + 1 - zr, True), (2 - xr, xr != zr)):
        for col in (zc, zc + toward, zc - toward):
            inside = (col >= 0) & (col < TW) & live
            for f in (frame, 1 - frame):
                tiles.append(jnp.where(inside, f * 32 + row * TW + col, -2))
    return jnp.stack(tiles)


def swapped(first, second, lines):
    return column_swap(first, 0, lines), column_swap(second, 1, lines)


def from_rows(value):
    return [lax.ppermute(value, "y", [(i, (i + step) % 4) for i in range(4)]) for step in (1, 2, 3)]


def sum_of(*terms):
    total = terms[0].astype(jnp.float32)
    for term in terms[1:]:
        total = total + term.astype(jnp.float32)
    return total


def body(queries, keys, values, out_weight, teacher, block_lists):
    xf, xr, zr, zc = (lax.axis_index(axis) for axis in TILE_AXES)
    place = jnp.stack([xf, lax.axis_index("y"), lax.axis_index("core")]).astype(jnp.int32)

    kv_mine, kv_other, q_mine, q_other = prepare(place, queries, keys, values)

    def listed(head, frame):
        lists = lax.dynamic_index_in_dim(block_lists[:, 0], head, 0, keepdims=False)
        return jnp.any(lists[:, None] == slot_tiles(frame, xr, zr, zc)[None, :], axis=0)

    mask_row = jnp.pad(listed(1 - xf, 1 - xf).astype(jnp.bfloat16), (0, HD - SLOTS))
    message = jnp.concatenate(
        [kv_other.reshape(2 * TILE, HD), q_other, jnp.broadcast_to(mask_row[None], (16, HD))]
    )
    xf_got = lax.ppermute(message, "xf", SWAP)
    allowed = jnp.stack([listed(xf, xf), xf_got[3 * TILE, :SLOTS] > 0.5]).astype(jnp.int32)
    allowed = jnp.concatenate([allowed, jnp.broadcast_to(xf.astype(jnp.int32), (2, 1))], axis=1)

    pair = simple(pair_kernel, "pair", [shape(2, 2, TILE, HD)], kv_mine, xf_got)[0]
    row = lax.ppermute(pair, "zr", SWAP)
    third = lax.ppermute(row, ("xr", "zr"), [(0, 2), (3, 1)])
    own_windows = (pair, *swapped(pair, pair, ALL_LINES))
    row_windows = (row, *swapped(row, row, ALL_LINES))
    third_windows = (third, *swapped(third, third, MIDDLE_LINES))

    weight_heads = out_weight.reshape(2, HD, 8 * TILE)
    first_head = jnp.where(xf == 0, weight_heads[0], weight_heads[1])
    second_head = jnp.where(xf == 0, weight_heads[1], weight_heads[0])
    far_teacher = lax.ppermute(teacher, "core", SWAP)
    first_head, _ = lax.optimization_barrier((first_head, xf_got))
    pack = jnp.concatenate([jnp.concatenate([first_head, second_head]), teacher, far_teacher], axis=1)
    ring = [(i, (i + 1) % 4) for i in range(4)]
    up = lax.ppermute(pack, "y", ring)
    down = lax.ppermute(pack, "y", [(i, (i + 3) % 4) for i in range(4)])
    across = lax.ppermute(up, "y", ring)
    packs = [pack, up, across, down]

    own_weights, row_weights, *sums_before = forward(allowed, q_mine, xf_got, own_windows + row_windows)
    third_weights, own, other, spread, inverse, inverse_third = forward(
        allowed, q_mine, xf_got, third_windows, sums_before
    )

    gathered = lax.all_to_all(spread.reshape(8, TILE, HD), ("xf", "y"), 0, 0, tiled=True)
    partial_mine = project(place, gathered.reshape(2, 4, TILE, HD), packs)
    partial_other = lax.ppermute(partial_mine, "core", SWAP)
    student, grad_mine, grad_other = residue_grad(place, partial_mine, partial_other, packs)
    grad_got = lax.ppermute(grad_other, "xf", SWAP)

    common = (q_mine, xf_got, grad_mine, grad_got, own, other, inverse)
    common_third = common[:-1] + (inverse_third,)
    before = jnp.zeros((2, HD, TILE), jnp.float32)
    before, far, far_left, far_right = backward(common_third, before, third_weights, third_windows)
    before, part, part_left, part_right = backward(common, before, row_weights, row_windows)
    far_sum = simple(
        far_kernel, "far_sum", [shape(2, 2, TILE, HD)], far, *swapped(far_left, far_right, MIDDLE_LINES)
    )[0]
    third_back = lax.ppermute(far_sum, ("xr", "zr"), [(2, 0), (1, 3)])
    row_sum = simple(
        merge_kernel,
        "merge",
        [shape(2, 2, TILE, HD)],
        part,
        *swapped(part_left, part_right, ALL_LINES),
        third_back,
    )[0]
    row_back = lax.ppermute(row_sum, "zr", SWAP)
    row_back = simple(widen_kernel, "widen", [shape(2, 2, TILE, HD, dtype=jnp.float32)], row_back, flops=30_000_000_000)[0]
    before, _ = lax.optimization_barrier((before, row_sum))
    grad_query, near, near_left, near_right = backward(common, before, own_weights, own_windows, last=True)
    from_right, from_left = swapped(near_left, near_right, ALL_LINES)
    sums = (near, from_right, from_left, row_back, grad_query)
    frame_sum = simple(frame_kernel, "frame_sum", [shape(3, TILE, HD)], *sums)[0]
    xf_back = lax.ppermute(frame_sum, "xf", SWAP)
    grad_queries, grad_keys, grad_values = simple(
        join_kernel, "join", [shape(TILE, TILE)] * 3, *sums, xf_back, place=place
    )
    return student, grad_queries, grad_keys, grad_values


def solution(mesh):
    split = Mesh(mesh.devices.reshape(2, 2, 2, 8, 4, 2), TILE_AXES + HEAD_AXES)
    both = P(TILE_AXES, HEAD_AXES)
    return jax.shard_map(
        body,
        mesh=split,
        in_specs=(both, both, both, P(HEAD_AXES, None), both, P(HEAD_AXES, TILE_AXES, None)),
        out_specs=(both, both, both, both),
        check_vma=False,
    )
```
